128 devices in a mesh: band: 32 (over z, x, y_lo), space: 4 (over y_hi, core).
Axes of the slice: x: 4, y: 4 (y_hi: 2, y_lo: 2; y = y_hi * 2 + y_lo), z: 4, core: 2. Of those that a mesh axis runs over, the one named last changes fastest.
Arguments:
- panels: float32 [3, 64, 32, 128, 128], P(None, 'band', 'space'), may hold values from -6 to 6
- potential: float32 [32, 128, 128], P('space'), may hold values from -8 to 0
- block_index: int32 [1], replicated, may hold values from 0 to 2
Outputs:
- filtered: float32 [64, 32, 128, 128], P('band', 'space')
- updated: float32 [3, 64, 32, 128, 128], P(None, 'band', 'space')
The draws below stay inside these ranges and needn't reach their ends.
All inputs are finite; a program needn't handle non-finite values.
Results may differ from the reference program's by a relative error of at most 0.000071.
Values sent between devices are 32-bit elements; how exact they have to be, the bound alone decides.
No kernel may reach another device: no remote copies, remote signals or barrier semaphores. Data moves between devices by JAX's collectives and lax.ppermute only.
A program may use at most 192 MiB of HBM per device.

```python
import jax
import jax.numpy as jnp
from jax import lax

PANEL = 64
NPANELS = 3
NX = 128
NY = 128
NZ = 32


def block_levels(key, extent, split, smallest, top_value):
    def one(dim, blocks):
        draws = jax.random.uniform(jax.random.fold_in(jax.random.fold_in(key, 6), dim), (blocks,), jnp.float32, smallest / len(split), top_value / len(split))
        return jnp.repeat(jnp.exp(draws), extent[dim] // blocks).reshape((-1,) + (1,) * (len(extent) - dim - 1))

    gain = one(*split[0])
    for cut in split[1:]:
        gain = gain * one(*cut)
    return gain


def scatter_about(rng, shape, width, reach, cuts=(), kind=jnp.bfloat16):
    result = jax.random.normal(rng, shape, jnp.float32) * width
    if len(cuts) > 0:
        result = block_levels(rng, shape, cuts, -0.22, 0.18) * result
    return jnp.clip(result, min=-reach, max=reach).astype(kind)


def setup_inputs(seed: int = 0) -> dict:
    arg_keys = jax.random.split(jax.random.key(seed), 4)
    panels = scatter_about(arg_keys[0], (NPANELS, PANEL, NZ, NX, NY), 1.0, 6.0, ((1, 32), (2, 4)), jnp.float32)
    potential = jnp.clip(-8.0 + 8.0 * jax.random.uniform(arg_keys[1], (NZ, NX, NY), jnp.float32) ** block_levels(arg_keys[1], (NZ, NX, NY), ((0, 4),), -0.2, 0.2), -8.0, 0.0)
    block_index = jax.random.randint(arg_keys[2], (1,), 0, NPANELS).astype(jnp.int32)
    return dict(panels=panels, potential=potential, block_index=block_index)


stencil_weights = (-5369.0 / 1800.0, 12.0 / 7.0, -15.0 / 56.0, 10.0 / 189.0, -1.0 / 112.0, 2.0 / 1925.0, -1.0 / 16632.0)
stencil_reach = 6
kinetic_factor = -0.5 / 0.25
centre_value = 32.25
half_width = 10.75


def wrap_planes(field):
    return jnp.concatenate([field[:, -stencil_reach:], field, field[:, :stencil_reach]], axis=1)


def hamiltonian(padded, potential):
    plane_count = padded.shape[1] - 2 * stencil_reach
    centre = padded[:, stencil_reach:stencil_reach + plane_count]
    laplace = 3.0 * stencil_weights[0] * centre
    for offset in range(1, stencil_reach + 1):
        upper = padded[:, stencil_reach + offset:stencil_reach + offset + plane_count]
        lower = padded[:, stencil_reach - offset:stencil_reach - offset + plane_count]
        across = jnp.roll(centre, offset, 2) + jnp.roll(centre, -offset, 2)
        along = jnp.roll(centre, offset, 3) + jnp.roll(centre, -offset, 3)
        laplace = laplace + stencil_weights[offset] * (upper + lower + across + along)
    return kinetic_factor * laplace + potential[None] * centre


def chebyshev(block_rows, potential):
    applied = hamiltonian(wrap_planes(block_rows), potential)
    first_term = (applied - centre_value * block_rows) / half_width
    second = hamiltonian(wrap_planes(first_term), potential)
    return 2.0 * (second - centre_value * first_term) / half_width - block_rows


def reference(panels, potential, block_index):
    block_rows = lax.dynamic_index_in_dim(panels, block_index[0].astype(jnp.int32), 0, keepdims=False)
    filtered = chebyshev(block_rows, potential)
    cell_count = NZ * NX * NY
    flat_filtered = filtered.reshape(PANEL, cell_count)
    stacked = panels.reshape(NPANELS, PANEL, cell_count)

    def update(one_panel):
        correlation = lax.dot_general(one_panel, flat_filtered, (((1,), (1,)), ((), ())), precision=lax.Precision.HIGHEST, preferred_element_type=jnp.float32) / cell_count
        return one_panel - jnp.dot(correlation, flat_filtered, precision=lax.Precision.HIGHEST, preferred_element_type=jnp.float32)

    updated = lax.map(update, stacked).reshape(panels.shape)
    return filtered, updated
```

```python
import jax
import jax.numpy as jnp
from jax import lax
from jax.experimental import pallas as pl
from jax.experimental.pallas import tpu as pltpu
from jax.sharding import PartitionSpec as P

stencil_weights = (
    -5369.0 / 1800.0,
    12.0 / 7.0,
    -15.0 / 56.0,
    10.0 / 189.0,
    -1.0 / 112.0,
    2.0 / 1925.0,
    -1.0 / 16632.0,
)
reach = 6
kinetic_factor = -0.5 / 0.25
centre_value = 32.25
half_width = 10.75
vmem_bytes = 48 * 1024 * 1024


def stencil_kernel(second, lo_ref, mid_ref, hi_ref, pot_ref, *rest):
    if second:
        before_ref, out_ref, pad_ref = rest
    else:
        out_ref, pad_ref = rest
    planes = mid_ref.shape[1]
    rows, columns = mid_ref.shape[2:]
    pad_ref[0:reach] = lo_ref[0]
    pad_ref[reach : reach + planes] = mid_ref[0]
    pad_ref[reach + planes : 2 * reach + planes] = hi_ref[0]

    def one_plane(z, carry):
        centre = pad_ref[z + reach]
        laplace = 3.0 * stencil_weights[0] * centre
        for k in range(1, reach + 1):
            total = pad_ref[z + reach + k] + pad_ref[z + reach - k]
            total = total + (pltpu.roll(centre, k, 0) + pltpu.roll(centre, rows - k, 0))
            total = total + (pltpu.roll(centre, k, 1) + pltpu.roll(centre, columns - k, 1))
            laplace = laplace + stencil_weights[k] * total
        applied = kinetic_factor * laplace + pot_ref[z] * centre
        term = (applied - centre_value * centre) * (1.0 / half_width)
        if second:
            term = 2.0 * term - before_ref[0, z]
        out_ref[0, z] = term
        return carry

    lax.fori_loop(0, planes, one_plane, 0)


def stencil(lo, mid, hi, potential, before=None):
    bands, planes, rows, columns = mid.shape

    def field(depth):
        return pl.BlockSpec((1, depth, rows, columns), lambda b: (b, 0, 0, 0))

    operands = [lo, mid, hi, potential] + ([] if before is None else [before])
    specs = [field(reach), field(planes), field(reach)]
    specs += [pl.BlockSpec((planes, rows, columns), lambda b: (0, 0, 0))]
    specs += [] if before is None else [field(planes)]

    def body(*refs):
        stencil_kernel(before is not None, *refs)

    return pl.pallas_call(
        body,
        grid=(bands,),
        in_specs=specs,
        out_specs=field(planes),
        out_shape=jax.ShapeDtypeStruct(mid.shape, jnp.float32),
        scratch_shapes=[pltpu.VMEM((planes + 2 * reach, rows, columns), jnp.float32)],
        compiler_params=pltpu.CompilerParams(vmem_limit_bytes=vmem_bytes),
        cost_estimate=pl.CostEstimate(flops=50 * mid.size, bytes_accessed=16 * mid.size, transcendentals=0),
        name="stencil",
    )(*operands)


def split(value):
    high = value.astype(jnp.bfloat16)
    low = (value - high.astype(jnp.float32)).astype(jnp.bfloat16)
    return high, low


def gram_kernel(panel_ref, block_ref, out_ref):
    segments = 32
    rows = panel_ref.shape[0] // segments
    bands = block_ref.shape[0] // segments
    half = segments // 2
    contract = (((1,), (1,)), ((), ()))

    def one(j, total):
        def pair(ref, count):
            first = ref[pl.ds(j, count, segments), :]
            other = ref[pl.ds(j + half, count, segments), :]
            return jnp.concatenate([first, other], axis=1)

        panel_high, panel_low = split(pair(panel_ref, rows))
        block_high, block_low = split(pair(block_ref, bands))
        both = jnp.concatenate([block_high, block_low], axis=0)
        wide = lax.dot_general(panel_high, both, contract, preferred_element_type=jnp.float32)
        narrow = lax.dot_general(panel_low, block_high, contract, preferred_element_type=jnp.float32)
        return total + (wide[:, :bands] + (wide[:, bands:] + narrow))

    out_ref[...] = lax.fori_loop(0, half, one, jnp.zeros((rows, bands), jnp.float32))


def gram(panel_rows, block_rows):
    rows, bands = panel_rows.shape[0] // 32, block_rows.shape[0] // 32
    return pl.pallas_call(
        gram_kernel,
        out_shape=jax.ShapeDtypeStruct((rows, bands), jnp.float32),
        compiler_params=pltpu.CompilerParams(vmem_limit_bytes=vmem_bytes),
        cost_estimate=pl.CostEstimate(
            flops=6 * rows * bands * 4096, bytes_accessed=4 * (panel_rows.size + block_rows.size), transcendentals=0
        ),
        name="gram",
    )(panel_rows, block_rows)


def update_kernel(corr_ref, block_ref, panel_ref, out_ref):
    segments = 32
    rows = panel_ref.shape[0] // segments
    bands = block_ref.shape[0] // segments
    half = segments // 2
    corr_high, corr_low = split(corr_ref[...])
    left = jnp.concatenate([corr_high, corr_high, corr_low], axis=1)

    def one(j, carry):
        pair = jnp.concatenate(
            [block_ref[pl.ds(j, bands, segments), :], block_ref[pl.ds(j + half, bands, segments), :]], axis=1
        )
        high, low = split(pair)
        product = jnp.dot(left, jnp.concatenate([high, low, high], axis=0), preferred_element_type=jnp.float32)
        for start, part in ((j, product[:, :128]), (j + half, product[:, 128:])):
            place = pl.ds(start, rows, segments)
            out_ref[place, :] = panel_ref[place, :] - part
        return carry

    lax.fori_loop(0, half, one, 0)


def update(correlation, block_rows, panel_rows):
    rows, bands = correlation.shape
    return pl.pallas_call(
        update_kernel,
        out_shape=jax.ShapeDtypeStruct(panel_rows.shape, jnp.float32),
        compiler_params=pltpu.CompilerParams(vmem_limit_bytes=vmem_bytes),
        cost_estimate=pl.CostEstimate(
            flops=6 * rows * bands * 4096, bytes_accessed=8 * panel_rows.size, transcendentals=0
        ),
        name="update",
    )(correlation, block_rows, panel_rows)


def halos(field):
    size, planes = lax.axis_size("space"), field.shape[1]
    up = [(i, (i + 1) % size) for i in range(size)]
    down = [(j, i) for i, j in up]
    before = lax.ppermute(field[:, planes - reach :], "space", up)
    after = lax.ppermute(field[:, :reach], "space", down)
    return before, after


def summed(value):
    size = lax.axis_size("space")
    parts = [value]
    for step in range(1, size):
        parts.append(lax.ppermute(value, "space", [(i, (i + step) % size) for i in range(size)]))
    value = sum(parts[1:], parts[0])
    bands = lax.axis_size("band")
    for stride, length in ((1, 2), (2, 4), (8, 4)):
        parts = [value]
        for step in range(1, length):
            moves = []
            for i in range(bands):
                digit = i // stride % length
                moves.append((i, i + ((digit + step) % length - digit) * stride))
            parts.append(lax.ppermute(value, "band", moves))
        value = sum(parts[1:], parts[0])
    return value


def shards(panels, potential, block_index):
    count, own = panels.shape[:2]
    bands = lax.axis_size("band")
    cell_count = lax.axis_size("space") * potential.size
    lanes = panels.shape[-1]
    chunked = panels.reshape(count * own, bands, -1, lanes)
    sent = jnp.swapaxes(chunked, 0, 1)
    panel_rows = lax.all_to_all(sent, "band", 0, 0, tiled=True).reshape(-1, lanes)

    block = lax.dynamic_index_in_dim(panels, block_index[0], 0, keepdims=False)
    before, after = halos(block)
    first = stencil(before, block, after, potential)
    before, after = halos(first)
    filtered = stencil(before, first, after, potential, block)

    own_chunks = jnp.swapaxes(filtered.reshape(own, bands, -1, lanes), 0, 1)
    block_rows = lax.all_to_all(own_chunks, "band", 0, 0, tiled=True).reshape(-1, lanes)

    partial = gram(panel_rows, block_rows)
    correlation = summed(partial) * (1.0 / cell_count)
    fresh = update(correlation, block_rows, panel_rows).reshape(sent.shape)
    home = lax.all_to_all(fresh, "band", 0, 0, tiled=True)
    updated = jnp.swapaxes(home, 0, 1).reshape(panels.shape)
    return filtered, updated


def solution(mesh):
    return jax.shard_map(
        shards,
        mesh=mesh,
        in_specs=(P(None, "band", "space", None, None), P("space", None, None), P()),
        out_specs=(P("band", "space", None, None), P(None, "band", "space", None, None)),
        check_vma=False,
    )
```

```python
import jax
import jax.numpy as jnp
from jax import lax
from jax.experimental import pallas as pl
from jax.experimental.pallas import tpu as pltpu
from jax.sharding import Mesh, PartitionSpec as P

stencil_weights = (
    -5369.0 / 1800.0,
    12.0 / 7.0,
    -15.0 / 56.0,
    10.0 / 189.0,
    -1.0 / 112.0,
    2.0 / 1925.0,
    -1.0 / 16632.0,
)
reach = 6
kinetic_factor = -0.5 / 0.25
centre_value = 32.25
half_width = 10.75
vmem_bytes = 48 * 1024 * 1024


def stencil_kernel(second, lo_ref, mid_ref, hi_ref, pot_ref, *rest):
    if second:
        before_ref, out_ref, chunk_ref, pad_ref = rest
    else:
        out_ref, pad_ref = rest
    planes, rows, columns = mid_ref.shape[1:]
    pad_ref[0:reach] = lo_ref[0]
    pad_ref[reach : reach + planes] = mid_ref[0]
    pad_ref[reach + planes : 2 * reach + planes] = hi_ref[0]

    def one_plane(z, carry):
        centre = pad_ref[z + reach]
        laplace = 3.0 * stencil_weights[0] * centre
        for k in range(1, reach + 1):
            total = pad_ref[z + reach + k] + pad_ref[z + reach - k]
            total = total + (pltpu.roll(centre, k, 0) + pltpu.roll(centre, rows - k, 0))
            total = total + (pltpu.roll(centre, k, 1) + pltpu.roll(centre, columns - k, 1))
            laplace = laplace + stencil_weights[k] * total
        applied = kinetic_factor * laplace + pot_ref[z] * centre
        term = (applied - centre_value * centre) * (1.0 / half_width)
        if second:
            term = 2.0 * term - before_ref[0, z]
            cuts, copies, _, height, _ = chunk_ref.shape
            for i in range(cuts // planes):
                for j in range(copies):
                    chunk_ref[z * (cuts // planes) + i, j, 0] = term[i * height : (i + 1) * height]
        out_ref[0, z] = term
        return carry

    lax.fori_loop(0, planes, one_plane, 0)


def stencil(lo, mid, hi, potential, before=None, chunks=None):
    bands, planes, rows, columns = mid.shape

    def field(depth):
        return pl.BlockSpec((1, depth, rows, columns), lambda b: (b, 0, 0, 0))

    second = before is not None
    weight = 50 if second else 5000000
    operands = [lo, mid, hi, potential]
    specs = [field(reach), field(planes), field(reach)]
    specs += [pl.BlockSpec((planes, rows, columns), lambda b: (0, 0, 0))]
    out_specs, out_shape = [field(planes)], [jax.ShapeDtypeStruct(mid.shape, jnp.float32)]
    if second:
        operands.append(before)
        specs.append(field(planes))
        spots, copies = chunks
        height = planes * rows // spots
        out_specs.append(pl.BlockSpec((spots, copies, 1, height, columns), lambda b: (0, 0, b, 0, 0)))
        out_shape.append(jax.ShapeDtypeStruct((spots, copies, bands, height, columns), jnp.float32))

    def body(*refs):
        stencil_kernel(second, *refs)

    return pl.pallas_call(
        body,
        grid=(bands,),
        in_specs=specs,
        out_specs=out_specs,
        out_shape=out_shape,
        scratch_shapes=[pltpu.VMEM((planes + 2 * reach, rows, columns), jnp.float32)],
        compiler_params=pltpu.CompilerParams(vmem_limit_bytes=vmem_bytes),
        cost_estimate=pl.CostEstimate(flops=weight * mid.size, bytes_accessed=16 * mid.size, transcendentals=0),
        name="stencil",
    )(*operands)


def split(value):
    high = value.astype(jnp.bfloat16)
    low = (value - high.astype(jnp.float32)).astype(jnp.bfloat16)
    return high, low


def pair(ref, j):
    rows, segments = ref.shape[:2]
    flat = ref.reshape(rows * segments, ref.shape[2])
    first = flat[pl.ds(j, rows, segments), :]
    other = flat[pl.ds(j + segments // 2, rows, segments), :]
    return jnp.concatenate([first, other], axis=1)


def gram_kernel(panel_ref, block_ref, out_ref):
    rows, segments = panel_ref.shape[:2]
    bands = block_ref.shape[0]
    contract = (((1,), (1,)), ((), ()))

    def one(j, total):
        panel_high, panel_low = split(pair(panel_ref, j))
        block_high, block_low = split(pair(block_ref, j))
        both = jnp.concatenate([block_high, block_low], axis=0)
        wide = lax.dot_general(both, panel_high, contract, preferred_element_type=jnp.float32)
        narrow = lax.dot_general(block_high, panel_low, contract, preferred_element_type=jnp.float32)
        return total + (wide[:bands] + (wide[bands:] + narrow))

    out_ref[...] = lax.fori_loop(0, segments // 2, one, jnp.zeros((bands, rows), jnp.float32), unroll=4)


def gram(panel_rows, block_rows):
    rows, bands = panel_rows.shape[0], block_rows.shape[0]
    return pl.pallas_call(
        gram_kernel,
        out_shape=jax.ShapeDtypeStruct((bands, rows), jnp.float32),
        compiler_params=pltpu.CompilerParams(vmem_limit_bytes=vmem_bytes),
        cost_estimate=pl.CostEstimate(
            flops=6 * bands * panel_rows.size, bytes_accessed=4 * (panel_rows.size + block_rows.size), transcendentals=0
        ),
        name="gram",
    )(panel_rows, block_rows)


def update_kernel(scale, sums_ref, block_ref, panel_ref, out_ref):
    rows, segments, lanes = panel_ref.shape
    total = sums_ref[0]
    for i in range(1, sums_ref.shape[0]):
        total = total + sums_ref[i]
    corr_high, corr_low = split((total * scale).T)
    left = jnp.concatenate([corr_high, corr_high, corr_low], axis=1)
    flat_panel = panel_ref.reshape(rows * segments, lanes)
    flat_out = out_ref.reshape(rows * segments, lanes)
    half = segments // 2

    def one(j, carry):
        high, low = split(pair(block_ref, j))
        product = jnp.dot(left, jnp.concatenate([high, low, high], axis=0), preferred_element_type=jnp.float32)
        for start, part in ((j, product[:, :lanes]), (j + half, product[:, lanes:])):
            place = pl.ds(start, rows, segments)
            flat_out[place, :] = flat_panel[place, :] - part
        return carry

    lax.fori_loop(0, half, one, 0, unroll=4)


def update(sums, scale, block_rows, panel_rows):
    def body(*refs):
        update_kernel(scale, *refs)

    return pl.pallas_call(
        body,
        out_shape=jax.ShapeDtypeStruct(panel_rows.shape, jnp.float32),
        compiler_params=pltpu.CompilerParams(vmem_limit_bytes=vmem_bytes),
        cost_estimate=pl.CostEstimate(
            flops=6 * block_rows.shape[0] * panel_rows.size, bytes_accessed=8 * panel_rows.size, transcendentals=0
        ),
        name="update",
    )(sums, block_rows, panel_rows)


def halos(field):
    planes = field.shape[1]
    up = [(i, (i + 1) % 4) for i in range(4)]
    down = [(j, i) for i, j in up]
    before = lax.ppermute(field[:, planes - reach :], ("yh", "c"), up)
    after = lax.ppermute(field[:, :reach], ("yh", "c"), down)
    return before, after


def summed(partial, spots):
    parts = [partial]
    for step in range(1, 4):
        parts.append(lax.ppermute(partial, ("yh", "c"), [(i, i ^ step) for i in range(4)]))
    partial = (parts[0] + parts[1]) + (parts[2] + parts[3])
    copies = jnp.broadcast_to(partial[None], (spots,) + partial.shape)
    return lax.all_to_all(copies, ("z", "x"), 0, 0, tiled=True)


def shards(panels, potential, block_index):
    count, own = panels.shape[:2]
    lanes = panels.shape[-1]
    spots = lax.axis_size("z") * lax.axis_size("x")
    cell_count = lax.axis_size("yh") * lax.axis_size("c") * potential.size

    block = lax.dynamic_index_in_dim(panels, block_index[0], 0, keepdims=False)
    before, after = halos(block)
    sent = jnp.swapaxes(panels.reshape(count * own, spots, -1, lanes), 0, 1)
    panel_rows = lax.all_to_all(sent, ("z", "x"), 0, 0, tiled=True)
    panel_rows = panel_rows.reshape((-1,) + sent.shape[2:])

    (first,) = stencil(before, block, after, potential)
    before, after = halos(first)
    filtered, chunks = stencil(before, first, after, potential, block, (spots, lax.axis_size("yl")))
    chunks, panel_rows = lax.optimization_barrier((chunks, panel_rows))
    chunks = chunks.reshape((-1,) + chunks.shape[2:])
    block_rows = lax.all_to_all(chunks, ("z", "x", "yl"), 0, 0, tiled=True)
    block_rows = block_rows.reshape((-1,) + chunks.shape[2:])

    sums = summed(gram(panel_rows, block_rows), spots)
    fresh = update(sums, 1.0 / cell_count, block_rows, panel_rows)
    home = lax.all_to_all(fresh.reshape(sent.shape), ("z", "x"), 0, 0, tiled=True)
    updated = jnp.swapaxes(home, 0, 1).reshape(panels.shape)
    return filtered, updated


def solution(mesh):
    fine = Mesh(mesh.devices.reshape(4, 4, 2, 2, 2), ("z", "x", "yl", "yh", "c"))
    band, space = ("z", "x", "yl"), ("yh", "c")
    return jax.shard_map(
        shards,
        mesh=fine,
        in_specs=(P(None, band, space, None, None), P(space, None, None), P()),
        out_specs=(P(band, space, None, None), P(None, band, space, None, None)),
        check_vma=False,
    )
```

```python
import jax
import jax.numpy as jnp
from jax import lax
from jax.experimental import pallas as pl
from jax.experimental.pallas import tpu as pltpu
from jax.sharding import Mesh, PartitionSpec as P

stencil_weights = (
    -5369.0 / 1800.0,
    12.0 / 7.0,
    -15.0 / 56.0,
    10.0 / 189.0,
    -1.0 / 112.0,
    2.0 / 1925.0,
    -1.0 / 16632.0,
)
reach = 6
kinetic_factor = -0.5 / 0.25
centre_value = 32.25
half_width = 10.75
vmem_bytes = 16 * 1024 * 1024


def inner_kernel(second, index_ref, panels_ref, pot_ref, *rest):
    if second:
        mid_ref, out_ref, held, held_pot, result_ref, before_ref, sems = rest
    else:
        out_ref, held, held_pot, result_ref, sems = rest
    bands, planes, rows, columns = held.shape
    block_ref = panels_ref.at[index_ref[0]]
    moves = [(pot_ref, held_pot)]
    for b in range(bands):
        moves.append(((mid_ref if second else block_ref).at[b], held.at[b]))
        if second:
            moves.append((block_ref.at[b], before_ref.at[b]))
    copies = [pltpu.make_async_copy(*move, sems.at[i]) for i, move in enumerate(moves)]
    for copy in copies:
        copy.start()
    copies[0].wait()
    scale = (2.0 if second else 1.0) / half_width
    leaving = []
    each = 2 if second else 1
    for b in range(bands):
        for copy in copies[1 + each * b : 1 + each * (b + 1)]:
            copy.wait()
        for z in range(planes):
            centre = held[b, z]
            laplace = 3.0 * stencil_weights[0] * centre
            for k in range(1, reach + 1):
                total = pltpu.roll(centre, k, 0) + pltpu.roll(centre, rows - k, 0)
                total = total + (pltpu.roll(centre, k, 1) + pltpu.roll(centre, columns - k, 1))
                if z + k < planes:
                    total = total + held[b, z + k]
                if z - k >= 0:
                    total = total + held[b, z - k]
                laplace = laplace + stencil_weights[k] * total
            applied = kinetic_factor * laplace + held_pot[z] * centre
            term = (applied - centre_value * centre) * scale
            if second:
                term = term - before_ref[b, z]
            result_ref[b, z] = term
        leaving.append(pltpu.make_async_copy(result_ref.at[b], out_ref.at[b], sems.at[5 + b]))
        leaving[b].start()
    for copy in leaving:
        copy.wait()


def outer_kernel(second, part_ref, lo_ref, hi_ref, out_ref, *rest):
    if second:
        chunk_ref, held, held_lo, held_hi, sems = rest
    else:
        held, held_lo, held_hi, sems = rest
    bands, planes, rows, columns = held.shape
    arrivals = []
    for b in range(bands):
        moves = [(part_ref.at[b], held.at[b]), (lo_ref.at[b], held_lo.at[b]), (hi_ref.at[b], held_hi.at[b])]
        copies = [pltpu.make_async_copy(*move, sems.at[3 * b + i]) for i, move in enumerate(moves)]
        for copy in copies:
            copy.start()
        arrivals.append(copies)
    scale = kinetic_factor * (2.0 if second else 1.0) / half_width
    strip = 16
    leaving = []
    for b in range(bands):
        for copy in arrivals[b]:
            copy.wait()

        def one(i, carry, b=b):
            place = pl.ds(pl.multiple_of(i * strip, strip), strip)
            low = [held_lo[b, j, place] for j in range(reach)]
            high = [held_hi[b, j, place] for j in range(reach)]
            for z in range(planes):
                total = held[b, z, place]
                for k in range(1, reach + 1):
                    if z + k >= planes:
                        total = total + (scale * stencil_weights[k]) * high[z + k - planes]
                    if z - k < 0:
                        total = total + (scale * stencil_weights[k]) * low[reach + z - k]
                held[b, z, place] = total
            return carry

        lax.fori_loop(0, rows // strip, one, 0)
        moves = [(held.at[b], out_ref.at[b])]
        if second:
            copies, spots, _, height, _ = chunk_ref.shape
            source = held.at[b].reshape(spots, height, columns)
            moves += [(source, chunk_ref.at[j, :, b]) for j in range(copies)]
        for i, move in enumerate(moves):
            copy = pltpu.make_async_copy(*move, sems.at[3 * bands + 3 * b + i])
            copy.start()
            leaving.append(copy)
    for copy in leaving:
        copy.wait()


hbm = pl.BlockSpec(memory_space=pltpu.HBM)
INNER_WEIGHT = 50
OUTER_WEIGHT = 100000


def inner(index, panels, potential, mid=None):
    shape = panels.shape[1:]
    second = mid is not None
    operands = [panels, potential] + ([mid] if second else [])
    held = pltpu.VMEM(shape, jnp.float32)
    scratch = [held, pltpu.VMEM(shape[1:], jnp.float32), held] + ([held] if second else [])

    def body(*refs):
        inner_kernel(second, *refs)

    size = potential.size * shape[0]
    return pl.pallas_call(
        body,
        in_specs=[pl.BlockSpec(memory_space=pltpu.SMEM)] + [hbm] * len(operands),
        out_specs=hbm,
        out_shape=jax.ShapeDtypeStruct(shape, jnp.float32),
        scratch_shapes=scratch + [pltpu.SemaphoreType.DMA((5 + shape[0],))],
        compiler_params=pltpu.CompilerParams(vmem_limit_bytes=vmem_bytes),
        cost_estimate=pl.CostEstimate(
            flops=(50 if second else INNER_WEIGHT) * size, bytes_accessed=12 * size, transcendentals=0
        ),
        name="inner",
    )(index, *operands)


def outer(part, lo, hi, chunks=None):
    bands, planes, rows, columns = part.shape
    second = chunks is not None
    weight = 10 if second else OUTER_WEIGHT
    out_shape = [jax.ShapeDtypeStruct(part.shape, jnp.float32)]
    if second:
        copies, spots = chunks
        out_shape.append(jax.ShapeDtypeStruct((copies, spots, bands, planes * rows // spots, columns), jnp.float32))
    halo = pltpu.VMEM((bands, reach, rows, columns), jnp.float32)

    def body(*refs):
        outer_kernel(second, *refs)

    return pl.pallas_call(
        body,
        in_specs=[hbm] * 3,
        out_specs=[hbm] * len(out_shape),
        out_shape=out_shape,
        scratch_shapes=[pltpu.VMEM(part.shape, jnp.float32), halo, halo, pltpu.SemaphoreType.DMA((6 * bands,))],
        compiler_params=pltpu.CompilerParams(vmem_limit_bytes=vmem_bytes),
        cost_estimate=pl.CostEstimate(flops=weight * part.size, bytes_accessed=16 * part.size, transcendentals=0),
        name="outer",
    )(part, lo, hi)


def prepare_kernel(index_ref, panel_ref, sent_ref, low_ref, high_ref):
    bands, planes, rows, columns = panel_ref.shape[1:]
    spots, _, height, _ = sent_ref.shape
    for b in range(bands):
        for z in range(planes):
            for i in range(spots // planes):
                sent_ref[z * (spots // planes) + i, b] = panel_ref[0, b, z, i * height : (i + 1) * height]

    @pl.when(pl.program_id(0) == index_ref[0])
    def edges():
        low_ref[...] = panel_ref[0, :, 0:reach]
        high_ref[...] = panel_ref[0, :, planes - reach : planes]


def prepare(index, panels, spots):
    count, bands, planes, rows, columns = panels.shape
    height = planes * rows // spots
    edge = (bands, reach, rows, columns)
    whole = pl.BlockSpec(edge, lambda p: (0, 0, 0, 0))
    return pl.pallas_call(
        prepare_kernel,
        grid=(count,),
        in_specs=[
            pl.BlockSpec(memory_space=pltpu.SMEM),
            pl.BlockSpec((1, bands, planes, rows, columns), lambda p: (p, 0, 0, 0, 0)),
        ],
        out_specs=[pl.BlockSpec((spots, bands, height, columns), lambda p: (0, p, 0, 0)), whole, whole],
        out_shape=[
            jax.ShapeDtypeStruct((spots, count * bands, height, columns), jnp.float32),
            jax.ShapeDtypeStruct(edge, jnp.float32),
            jax.ShapeDtypeStruct(edge, jnp.float32),
        ],
        compiler_params=pltpu.CompilerParams(vmem_limit_bytes=vmem_bytes),
        cost_estimate=pl.CostEstimate(flops=0, bytes_accessed=8 * panels.size, transcendentals=0),
        name="prepare",
    )(index, panels)


def settle_kernel(panel_ref, change_ref, out_ref):
    for i in range(change_ref.shape[0]):
        out_ref[:, i] = panel_ref[:, i] - change_ref[i]


def settle(rows, change):
    count, spots = rows.shape[:2]
    step = spots // 4
    mine = pl.BlockSpec((count, step) + rows.shape[2:], lambda i: (0, i, 0, 0))
    return pl.pallas_call(
        settle_kernel,
        grid=(spots // step,),
        in_specs=[mine, pl.BlockSpec((step, count) + rows.shape[2:], lambda i: (i, 0, 0, 0))],
        out_specs=mine,
        out_shape=jax.ShapeDtypeStruct(rows.shape, jnp.float32),
        compiler_params=pltpu.CompilerParams(vmem_limit_bytes=vmem_bytes),
        cost_estimate=pl.CostEstimate(flops=rows.size, bytes_accessed=12 * rows.size, transcendentals=0),
        name="settle",
    )(rows, change)


def split(value):
    high = value.astype(jnp.bfloat16)
    low = (value - high.astype(jnp.float32)).astype(jnp.bfloat16)
    return high, low


def pair(ref, j):
    rows, segments = ref.shape[:2]
    flat = ref.reshape(rows * segments, ref.shape[2])
    first = flat[pl.ds(j, rows, segments), :]
    other = flat[pl.ds(j + segments // 2, rows, segments), :]
    return jnp.concatenate([first, other], axis=1)


def gram_kernel(panel_ref, block_ref, out_ref, total_ref):
    rows, segments = panel_ref.shape[:2]
    bands = block_ref.shape[0]
    contract = (((1,), (1,)), ((), ()))

    def one(j, total):
        panel_high, panel_low = split(pair(panel_ref, j))
        block_high, block_low = split(pair(block_ref, j))
        both = jnp.concatenate([panel_high, panel_low], axis=0)
        wide = lax.dot_general(both, block_high, contract, preferred_element_type=jnp.float32)
        narrow = lax.dot_general(panel_high, block_low, contract, preferred_element_type=jnp.float32)
        return total + (wide[:rows] + (wide[rows:] + narrow))

    @pl.when(pl.program_id(0) == 0)
    def clear():
        total_ref[...] = jnp.zeros_like(total_ref)

    total = lax.fori_loop(0, segments // 2, one, total_ref[...], unroll=4)
    total_ref[...] = total

    @pl.when(pl.program_id(0) == pl.num_programs(0) - 1)
    def store():
        out_ref[...] = jnp.concatenate([total[: rows // 2], total[rows // 2 :]], axis=1)


def gram(panel_rows, block_rows):
    rows, segments, lanes = panel_rows.shape
    bands = block_rows.shape[0]
    steps = 4

    def part(count):
        return pl.BlockSpec((count, segments // steps, lanes), lambda i: (0, i, 0))

    return pl.pallas_call(
        gram_kernel,
        grid=(steps,),
        in_specs=[part(rows), part(bands)],
        out_specs=pl.BlockSpec((rows // 2, 2 * bands), lambda i: (0, 0)),
        out_shape=jax.ShapeDtypeStruct((rows // 2, 2 * bands), jnp.float32),
        scratch_shapes=[pltpu.VMEM((rows, bands), jnp.float32)],
        compiler_params=pltpu.CompilerParams(vmem_limit_bytes=vmem_bytes),
        cost_estimate=pl.CostEstimate(
            flops=6 * bands * panel_rows.size, bytes_accessed=4 * (panel_rows.size + block_rows.size), transcendentals=0
        ),
        name="gram",
    )(panel_rows, block_rows)


def project_kernel(scale, sums_ref, block_ref, out_ref):
    rows, segments, lanes = out_ref.shape
    bands = block_ref.shape[0]
    total = sums_ref[0]
    for i in range(1, sums_ref.shape[0]):
        total = total + sums_ref[i]
    total = total * scale
    corr_high, corr_low = split(jnp.concatenate([total[:, :bands], total[:, bands:]], axis=0))
    left = jnp.concatenate([corr_high, corr_high, corr_low], axis=1)
    flat_out = out_ref.reshape(rows * segments, lanes)
    half = segments // 2

    def one(j, carry):
        high, low = split(pair(block_ref, j))
        product = jnp.dot(left, jnp.concatenate([high, low, high], axis=0), preferred_element_type=jnp.float32)
        flat_out[pl.ds(j, rows, segments), :] = product[:, :lanes]
        flat_out[pl.ds(j + half, rows, segments), :] = product[:, lanes:]
        return carry

    lax.fori_loop(0, half, one, 0, unroll=4)


def project(sums, scale, block_rows):
    rows = 2 * sums.shape[1]
    shape = (rows,) + block_rows.shape[1:]

    def body(*refs):
        project_kernel(scale, *refs)

    return pl.pallas_call(
        body,
        out_shape=jax.ShapeDtypeStruct(shape, jnp.float32),
        compiler_params=pltpu.CompilerParams(vmem_limit_bytes=vmem_bytes),
        cost_estimate=pl.CostEstimate(
            flops=6 * rows * block_rows.size, bytes_accessed=4 * (rows * 8192 + block_rows.size), transcendentals=0
        ),
        name="project",
    )(sums, block_rows)


plane_axes = ("x", "z")


def exchange(low, high):
    up = [(i, (i + 1) % 4) for i in range(4)]
    down = [(j, i) for i, j in up]
    return lax.ppermute(high, ("yh", "c"), up), lax.ppermute(low, ("yh", "c"), down)


def summed(partial, spots):
    parts = [partial]
    for step in range(1, 4):
        parts.append(lax.ppermute(partial, ("yh", "c"), [(i, i ^ step) for i in range(4)]))
    partial = (parts[0] + parts[1]) + (parts[2] + parts[3])
    copies = jnp.broadcast_to(partial[None], (spots,) + partial.shape)
    return lax.all_to_all(copies, plane_axes, 0, 0, tiled=True)


def shards(panels, potential, block_index):
    count, own = panels.shape[:2]
    lanes = panels.shape[-1]
    spots = lax.axis_size(plane_axes)
    cell_count = lax.axis_size("yh") * lax.axis_size("c") * potential.size

    planes = panels.shape[2]
    rows = panels.reshape(count * own, spots, -1, lanes)
    sent, low, high = prepare(block_index, panels, spots)
    before, after = exchange(low, high)
    panel_rows = lax.all_to_all(sent, plane_axes, 0, 0, tiled=True)
    panel_rows = panel_rows.reshape((-1,) + sent.shape[2:])

    (first,) = outer(inner(block_index, panels, potential), before, after)
    before, after = exchange(first[:, :reach], first[:, planes - reach :])
    part = inner(block_index, panels, potential, first)
    filtered, chunks = outer(part, before, after, (lax.axis_size("yl"), spots))
    chunks, panel_rows = lax.optimization_barrier((chunks, panel_rows))
    chunks = chunks.reshape((-1,) + chunks.shape[2:])
    block_rows = lax.all_to_all(
        chunks, ("yl",) + plane_axes, 0, 0, tiled=True
    )
    block_rows = block_rows.reshape((-1,) + chunks.shape[2:])

    sums = summed(gram(panel_rows, block_rows), spots)
    change = project(sums, 1.0 / cell_count, block_rows)
    home = lax.all_to_all(change.reshape(sent.shape), plane_axes, 0, 0, tiled=True)
    updated = settle(rows, home).reshape(panels.shape)
    return filtered, updated


def solution(mesh):
    fine = Mesh(mesh.devices.reshape(4, 4, 2, 2, 2), ("z", "x", "yl", "yh", "c"))
    band, space = ("z", "x", "yl"), ("yh", "c")
    return jax.shard_map(
        shards,
        mesh=fine,
        in_specs=(P(None, band, space, None, None), P(space, None, None), P()),
        out_specs=(P(band, space, None, None), P(None, band, space, None, None)),
        check_vma=False,
    )
```

```python
import jax
import jax.numpy as jnp
from jax import lax
from jax.experimental import pallas as pl
from jax.experimental.pallas import tpu as pltpu
from jax.sharding import Mesh, PartitionSpec as P

stencil_weights = (
    -5369.0 / 1800.0,
    12.0 / 7.0,
    -15.0 / 56.0,
    10.0 / 189.0,
    -1.0 / 112.0,
    2.0 / 1925.0,
    -1.0 / 16632.0,
)
reach = 6
kinetic_factor = -0.5 / 0.25
centre_value = 32.25
half_width = 10.75
vmem_bytes = 16 * 1024 * 1024


def inner_kernel(second, index_ref, panels_ref, pot_ref, *rest):
    if second:
        mid_ref, out_ref, held, held_pot, result_ref, before_ref, sems = rest
    else:
        out_ref, held, held_pot, result_ref, sems = rest
    bands, planes, rows, columns = held.shape
    block_ref = panels_ref.at[index_ref[0]]
    moves = [(pot_ref, held_pot)]
    for b in range(bands):
        moves.append(((mid_ref if second else block_ref).at[b], held.at[b]))
        if second:
            moves.append((block_ref.at[b], before_ref.at[b]))
    copies = [pltpu.make_async_copy(*move, sems.at[i]) for i, move in enumerate(moves)]
    for copy in copies:
        copy.start()
    copies[0].wait()
    scale = (2.0 if second else 1.0) / half_width
    leaving = []
    each = 2 if second else 1
    for b in range(bands):
        for copy in copies[1 + each * b : 1 + each * (b + 1)]:
            copy.wait()
        for z in range(planes):
            centre = held[b, z]
            laplace = 3.0 * stencil_weights[0] * centre
            for k in range(1, reach + 1):
                total = pltpu.roll(centre, k, 0) + pltpu.roll(centre, rows - k, 0)
                total = total + (pltpu.roll(centre, k, 1) + pltpu.roll(centre, columns - k, 1))
                if z + k < planes:
                    total = total + held[b, z + k]
                if z - k >= 0:
                    total = total + held[b, z - k]
                laplace = laplace + stencil_weights[k] * total
            applied = kinetic_factor * laplace + held_pot[z] * centre
            term = (applied - centre_value * centre) * scale
            if second:
                term = term - before_ref[b, z]
            result_ref[b, z] = term
        leaving.append(pltpu.make_async_copy(result_ref.at[b], out_ref.at[b], sems.at[5 + b]))
        leaving[b].start()
    for copy in leaving:
        copy.wait()


def outer_kernel(second, part_ref, lo_ref, hi_ref, out_ref, *rest):
    if second:
        chunk_ref, held, held_lo, held_hi, sems = rest
    else:
        held, held_lo, held_hi, sems = rest
    bands, planes, rows, columns = held.shape
    arrivals = []
    for b in range(bands):
        moves = [(part_ref.at[b], held.at[b]), (lo_ref.at[b], held_lo.at[b]), (hi_ref.at[b], held_hi.at[b])]
        copies = [pltpu.make_async_copy(*move, sems.at[3 * b + i]) for i, move in enumerate(moves)]
        for copy in copies:
            copy.start()
        arrivals.append(copies)
    scale = kinetic_factor * (2.0 if second else 1.0) / half_width
    strip = 16
    leaving = []
    for b in range(bands):
        for copy in arrivals[b]:
            copy.wait()

        def one(i, carry, b=b):
            place = pl.ds(pl.multiple_of(i * strip, strip), strip)
            low = [held_lo[b, j, place] for j in range(reach)]
            high = [held_hi[b, j, place] for j in range(reach)]
            for z in range(planes):
                total = held[b, z, place]
                for k in range(1, reach + 1):
                    if z + k >= planes:
                        total = total + (scale * stencil_weights[k]) * high[z + k - planes]
                    if z - k < 0:
                        total = total + (scale * stencil_weights[k]) * low[reach + z - k]
                held[b, z, place] = total
            return carry

        lax.fori_loop(0, rows // strip, one, 0)
        moves = [(held.at[b], out_ref.at[b])]
        if second:
            copies, spots, _, height, _ = chunk_ref.shape
            source = held.at[b].reshape(spots, height, columns)
            moves += [(source, chunk_ref.at[j, :, b]) for j in range(copies)]
        for i, move in enumerate(moves):
            copy = pltpu.make_async_copy(*move, sems.at[3 * bands + 3 * b + i])
            copy.start()
            leaving.append(copy)
    for copy in leaving:
        copy.wait()


hbm = pl.BlockSpec(memory_space=pltpu.HBM)
INNER_WEIGHT = 50
OUTER_WEIGHT = 100000


def inner(index, panels, potential, mid=None):
    shape = panels.shape[1:]
    second = mid is not None
    operands = [panels, potential] + ([mid] if second else [])
    held = pltpu.VMEM(shape, jnp.float32)
    scratch = [held, pltpu.VMEM(shape[1:], jnp.float32), held] + ([held] if second else [])

    def body(*refs):
        inner_kernel(second, *refs)

    size = potential.size * shape[0]
    return pl.pallas_call(
        body,
        in_specs=[pl.BlockSpec(memory_space=pltpu.SMEM)] + [hbm] * len(operands),
        out_specs=hbm,
        out_shape=jax.ShapeDtypeStruct(shape, jnp.float32),
        scratch_shapes=scratch + [pltpu.SemaphoreType.DMA((5 + shape[0],))],
        compiler_params=pltpu.CompilerParams(vmem_limit_bytes=vmem_bytes),
        cost_estimate=pl.CostEstimate(
            flops=(50 if second else INNER_WEIGHT) * size, bytes_accessed=12 * size, transcendentals=0
        ),
        name="inner",
    )(index, *operands)


def outer(part, lo, hi, chunks=None):
    bands, planes, rows, columns = part.shape
    second = chunks is not None
    weight = 10 if second else OUTER_WEIGHT
    out_shape = [jax.ShapeDtypeStruct(part.shape, jnp.float32)]
    if second:
        copies, spots = chunks
        out_shape.append(jax.ShapeDtypeStruct((copies, spots, bands, planes * rows // spots, columns), jnp.float32))
    halo = pltpu.VMEM((bands, reach, rows, columns), jnp.float32)

    def body(*refs):
        outer_kernel(second, *refs)

    return pl.pallas_call(
        body,
        in_specs=[hbm] * 3,
        out_specs=[hbm] * len(out_shape),
        out_shape=out_shape,
        scratch_shapes=[pltpu.VMEM(part.shape, jnp.float32), halo, halo, pltpu.SemaphoreType.DMA((6 * bands,))],
        compiler_params=pltpu.CompilerParams(vmem_limit_bytes=vmem_bytes),
        cost_estimate=pl.CostEstimate(flops=weight * part.size, bytes_accessed=16 * part.size, transcendentals=0),
        name="outer",
    )(part, lo, hi)


def prepare_kernel(index_ref, panels_ref, sent_ref, low_ref, high_ref, held, sems):
    count, bands, planes, rows, columns = held.shape
    spots, _, height, _ = sent_ref.shape
    arrivals = [pltpu.make_async_copy(panels_ref.at[p], held.at[p], sems.at[p]) for p in range(count)]
    for copy in arrivals:
        copy.start()
    leaving = []

    def leave(source, target):
        copy = pltpu.make_async_copy(source, target, sems.at[count + len(leaving)])
        copy.start()
        leaving.append(copy)

    for p in range(count):
        arrivals[p].wait()
        for b in range(bands):
            leave(held.at[p, b].reshape(spots, height, columns), sent_ref.at[:, p * bands + b])
    block = held.at[index_ref[0]]
    leave(block.at[:, 0:reach], low_ref)
    leave(block.at[:, planes - reach : planes], high_ref)
    for copy in leaving:
        copy.wait()


def prepare(index, panels, spots):
    count, bands, planes, rows, columns = panels.shape
    height = planes * rows // spots
    edge = jax.ShapeDtypeStruct((bands, reach, rows, columns), jnp.float32)
    return pl.pallas_call(
        prepare_kernel,
        in_specs=[pl.BlockSpec(memory_space=pltpu.SMEM), hbm],
        out_specs=[hbm] * 3,
        out_shape=[jax.ShapeDtypeStruct((spots, count * bands, height, columns), jnp.float32), edge, edge],
        scratch_shapes=[pltpu.VMEM(panels.shape, jnp.float32), pltpu.SemaphoreType.DMA((count + count * bands + 2,))],
        compiler_params=pltpu.CompilerParams(vmem_limit_bytes=62 * 1024 * 1024),
        cost_estimate=pl.CostEstimate(flops=0, bytes_accessed=8 * panels.size, transcendentals=0),
        name="prepare",
    )(index, panels)


def settle_kernel(panel_ref, change_ref, out_ref):
    for i in range(change_ref.shape[0]):
        out_ref[:, i] = panel_ref[:, i] - change_ref[i]


def settle(rows, change):
    count, spots = rows.shape[:2]
    step = spots // 2
    mine = pl.BlockSpec((count, step) + rows.shape[2:], lambda i: (0, i, 0, 0))
    return pl.pallas_call(
        settle_kernel,
        grid=(spots // step,),
        in_specs=[mine, pl.BlockSpec((step, count) + rows.shape[2:], lambda i: (i, 0, 0, 0))],
        out_specs=mine,
        out_shape=jax.ShapeDtypeStruct(rows.shape, jnp.float32),
        compiler_params=pltpu.CompilerParams(vmem_limit_bytes=vmem_bytes),
        cost_estimate=pl.CostEstimate(flops=rows.size, bytes_accessed=12 * rows.size, transcendentals=0),
        name="settle",
    )(rows, change)


def split(value):
    high = value.astype(jnp.bfloat16)
    low = (value - high.astype(jnp.float32)).astype(jnp.bfloat16)
    return high, low


def pair(ref, j):
    rows, segments = ref.shape[:2]
    flat = ref.reshape(rows * segments, ref.shape[2])
    first = flat[pl.ds(j, rows, segments), :]
    other = flat[pl.ds(j + segments // 2, rows, segments), :]
    return jnp.concatenate([first, other], axis=1)


def gram_kernel(panel_ref, block_ref, out_ref, total_ref):
    rows, segments = panel_ref.shape[:2]
    bands = block_ref.shape[0]
    contract = (((1,), (1,)), ((), ()))

    def one(j, total):
        panel_high, panel_low = split(pair(panel_ref, j))
        block_high, block_low = split(pair(block_ref, j))
        both = jnp.concatenate([panel_high, panel_low], axis=0)
        wide = lax.dot_general(both, block_high, contract, preferred_element_type=jnp.float32)
        narrow = lax.dot_general(panel_high, block_low, contract, preferred_element_type=jnp.float32)
        return total + (wide[:rows] + (wide[rows:] + narrow))

    @pl.when(pl.program_id(0) == 0)
    def clear():
        total_ref[...] = jnp.zeros_like(total_ref)

    total = lax.fori_loop(0, segments // 2, one, total_ref[...], unroll=4)
    total_ref[...] = total

    @pl.when(pl.program_id(0) == pl.num_programs(0) - 1)
    def store():
        out_ref[...] = jnp.concatenate([total[: rows // 2], total[rows // 2 :]], axis=1)


def gram(panel_rows, block_rows):
    rows, segments, lanes = panel_rows.shape
    bands = block_rows.shape[0]
    steps = 4

    def part(count):
        return pl.BlockSpec((count, segments // steps, lanes), lambda i: (0, i, 0))

    return pl.pallas_call(
        gram_kernel,
        grid=(steps,),
        in_specs=[part(rows), part(bands)],
        out_specs=pl.BlockSpec((rows // 2, 2 * bands), lambda i: (0, 0)),
        out_shape=jax.ShapeDtypeStruct((rows // 2, 2 * bands), jnp.float32),
        scratch_shapes=[pltpu.VMEM((rows, bands), jnp.float32)],
        compiler_params=pltpu.CompilerParams(vmem_limit_bytes=vmem_bytes),
        cost_estimate=pl.CostEstimate(
            flops=6 * bands * panel_rows.size, bytes_accessed=4 * (panel_rows.size + block_rows.size), transcendentals=0
        ),
        name="gram",
    )(panel_rows, block_rows)


def project_kernel(scale, sums_ref, block_ref, out_ref):
    rows, segments, lanes = out_ref.shape
    bands = block_ref.shape[0]
    total = sums_ref[0]
    for i in range(1, sums_ref.shape[0]):
        total = total + sums_ref[i]
    total = total * scale
    corr_high, corr_low = split(jnp.concatenate([total[:, :bands], total[:, bands:]], axis=0))
    left = jnp.concatenate([corr_high, corr_high, corr_low], axis=1)
    flat_out = out_ref.reshape(rows * segments, lanes)
    half = segments // 2

    def one(j, carry):
        high, low = split(pair(block_ref, j))
        product = jnp.dot(left, jnp.concatenate([high, low, high], axis=0), preferred_element_type=jnp.float32)
        flat_out[pl.ds(j, rows, segments), :] = product[:, :lanes]
        flat_out[pl.ds(j + half, rows, segments), :] = product[:, lanes:]
        return carry

    lax.fori_loop(0, half, one, 0, unroll=4)


def project(sums, scale, block_rows):
    rows = 2 * sums.shape[1]
    shape = (rows,) + block_rows.shape[1:]

    def body(*refs):
        project_kernel(scale, *refs)

    return pl.pallas_call(
        body,
        out_shape=jax.ShapeDtypeStruct(shape, jnp.float32),
        compiler_params=pltpu.CompilerParams(vmem_limit_bytes=vmem_bytes),
        cost_estimate=pl.CostEstimate(
            flops=6 * rows * block_rows.size, bytes_accessed=4 * (rows * 8192 + block_rows.size), transcendentals=0
        ),
        name="project",
    )(sums, block_rows)


plane_axes = ("x", "z")


def exchange(low, high):
    up = [(i, (i + 1) % 4) for i in range(4)]
    down = [(j, i) for i, j in up]
    return lax.ppermute(high, ("yh", "c"), up), lax.ppermute(low, ("yh", "c"), down)


def summed(partial, spots):
    parts = [partial]
    for step in range(1, 4):
        parts.append(lax.ppermute(partial, ("yh", "c"), [(i, i ^ step) for i in range(4)]))
    partial = (parts[0] + parts[1]) + (parts[2] + parts[3])
    copies = jnp.broadcast_to(partial[None], (spots,) + partial.shape)
    return lax.all_to_all(copies, plane_axes, 0, 0, tiled=True)


def shards(panels, potential, block_index):
    count, own = panels.shape[:2]
    lanes = panels.shape[-1]
    spots = lax.axis_size(plane_axes)
    cell_count = lax.axis_size("yh") * lax.axis_size("c") * potential.size

    planes = panels.shape[2]
    rows = panels.reshape(count * own, spots, -1, lanes)
    sent, low, high = prepare(block_index, panels, spots)
    before, after = exchange(low, high)
    panel_rows = lax.all_to_all(sent, plane_axes, 0, 0, tiled=True)
    panel_rows = panel_rows.reshape((-1,) + sent.shape[2:])

    (first,) = outer(inner(block_index, panels, potential), before, after)
    before, after = exchange(first[:, :reach], first[:, planes - reach :])
    part = inner(block_index, panels, potential, first)
    filtered, chunks = outer(part, before, after, (lax.axis_size("yl"), spots))
    chunks, panel_rows = lax.optimization_barrier((chunks, panel_rows))
    chunks = chunks.reshape((-1,) + chunks.shape[2:])
    block_rows = lax.all_to_all(
        chunks, ("yl",) + plane_axes, 0, 0, tiled=True
    )
    block_rows = block_rows.reshape((-1,) + chunks.shape[2:])

    sums = summed(gram(panel_rows, block_rows), spots)
    change = project(sums, 1.0 / cell_count, block_rows)
    home = lax.all_to_all(change.reshape(sent.shape), plane_axes, 0, 0, tiled=True)
    updated = settle(rows, home).reshape(panels.shape)
    return filtered, updated


def solution(mesh):
    fine = Mesh(mesh.devices.reshape(4, 4, 2, 2, 2), ("z", "x", "yl", "yh", "c"))
    band, space = ("z", "x", "yl"), ("yh", "c")
    return jax.shard_map(
        shards,
        mesh=fine,
        in_specs=(P(None, band, space, None, None), P(space, None, None), P()),
        out_specs=(P(band, space, None, None), P(None, band, space, None, None)),
        check_vma=False,
    )
```

```python
import jax
import jax.numpy as jnp
from jax import lax
from jax.experimental import pallas as pl
from jax.experimental.pallas import tpu as pltpu
from jax.sharding import Mesh, PartitionSpec as P

stencil_weights = (
    -5369.0 / 1800.0,
    12.0 / 7.0,
    -15.0 / 56.0,
    10.0 / 189.0,
    -1.0 / 112.0,
    2.0 / 1925.0,
    -1.0 / 16632.0,
)
reach = 6
kinetic_factor = -0.5 / 0.25
centre_value = 32.25
half_width = 10.75
vmem_bytes = 16 * 1024 * 1024


def inner_kernel(second, index_ref, panels_ref, pot_ref, *rest):
    if second:
        mid_ref, out_ref, held, held_pot, result_ref, before_ref, sems = rest
    else:
        out_ref, held, held_pot, result_ref, sems = rest
    bands, planes, rows, columns = held.shape
    block_ref = panels_ref.at[index_ref[0]]
    moves = [(pot_ref, held_pot)]
    for b in range(bands):
        moves.append(((mid_ref if second else block_ref).at[b], held.at[b]))
        if second:
            moves.append((block_ref.at[b], before_ref.at[b]))
    copies = [pltpu.make_async_copy(*move, sems.at[i]) for i, move in enumerate(moves)]
    for copy in copies:
        copy.start()
    copies[0].wait()
    scale = (2.0 if second else 1.0) / half_width
    leaving = []
    each = 2 if second else 1
    for b in range(bands):
        for copy in copies[1 + each * b : 1 + each * (b + 1)]:
            copy.wait()
        for z in range(planes):
            centre = held[b, z]
            laplace = 3.0 * stencil_weights[0] * centre
            for k in range(1, reach + 1):
                total = pltpu.roll(centre, k, 0) + pltpu.roll(centre, rows - k, 0)
                total = total + (pltpu.roll(centre, k, 1) + pltpu.roll(centre, columns - k, 1))
                if z + k < planes:
                    total = total + held[b, z + k]
                if z - k >= 0:
                    total = total + held[b, z - k]
                laplace = laplace + stencil_weights[k] * total
            applied = kinetic_factor * laplace + held_pot[z] * centre
            term = (applied - centre_value * centre) * scale
            if second:
                term = term - before_ref[b, z]
            result_ref[b, z] = term
        leaving.append(pltpu.make_async_copy(result_ref.at[b], out_ref.at[b], sems.at[5 + b]))
        leaving[b].start()
    for copy in leaving:
        copy.wait()


def outer_kernel(second, part_ref, lo_ref, hi_ref, out_ref, *rest):
    if second:
        chunk_ref, held, held_lo, held_hi, sems = rest
    else:
        held, held_lo, held_hi, sems = rest
    bands, planes, rows, columns = held.shape
    arrivals = []
    for b in range(bands):
        moves = [(part_ref.at[b], held.at[b]), (lo_ref.at[b], held_lo.at[b]), (hi_ref.at[b], held_hi.at[b])]
        copies = [pltpu.make_async_copy(*move, sems.at[3 * b + i]) for i, move in enumerate(moves)]
        for copy in copies:
            copy.start()
        arrivals.append(copies)
    scale = kinetic_factor * (2.0 if second else 1.0) / half_width
    strip = 16
    leaving = []
    for b in range(bands):
        for copy in arrivals[b]:
            copy.wait()

        def one(i, carry, b=b):
            place = pl.ds(pl.multiple_of(i * strip, strip), strip)
            low = [held_lo[b, j, place] for j in range(reach)]
            high = [held_hi[b, j, place] for j in range(reach)]
            for z in range(planes):
                total = held[b, z, place]
                for k in range(1, reach + 1):
                    if z + k >= planes:
                        total = total + (scale * stencil_weights[k]) * high[z + k - planes]
                    if z - k < 0:
                        total = total + (scale * stencil_weights[k]) * low[reach + z - k]
                held[b, z, place] = total
            return carry

        lax.fori_loop(0, rows // strip, one, 0)
        moves = [(held.at[b], out_ref.at[b])]
        if second:
            copies, spots, _, height, _ = chunk_ref.shape
            source = held.at[b].reshape(spots, height, columns)
            moves += [(source, chunk_ref.at[j, :, b]) for j in range(copies)]
        for i, move in enumerate(moves):
            copy = pltpu.make_async_copy(*move, sems.at[3 * bands + 3 * b + i])
            copy.start()
            leaving.append(copy)
    for copy in leaving:
        copy.wait()


hbm = pl.BlockSpec(memory_space=pltpu.HBM)
INNER_WEIGHT = 50
OUTER_WEIGHT = 100000


def inner(index, panels, potential, mid=None):
    shape = panels.shape[1:]
    second = mid is not None
    operands = [panels, potential] + ([mid] if second else [])
    held = pltpu.VMEM(shape, jnp.float32)
    scratch = [held, pltpu.VMEM(shape[1:], jnp.float32), held] + ([held] if second else [])

    def body(*refs):
        inner_kernel(second, *refs)

    size = potential.size * shape[0]
    return pl.pallas_call(
        body,
        in_specs=[pl.BlockSpec(memory_space=pltpu.SMEM)] + [hbm] * len(operands),
        out_specs=hbm,
        out_shape=jax.ShapeDtypeStruct(shape, jnp.float32),
        scratch_shapes=scratch + [pltpu.SemaphoreType.DMA((5 + shape[0],))],
        compiler_params=pltpu.CompilerParams(vmem_limit_bytes=vmem_bytes),
        cost_estimate=pl.CostEstimate(
            flops=(50 if second else INNER_WEIGHT) * size, bytes_accessed=12 * size, transcendentals=0
        ),
        name="inner",
    )(index, *operands)


def outer(part, lo, hi, chunks=None):
    bands, planes, rows, columns = part.shape
    second = chunks is not None
    weight = 10 if second else OUTER_WEIGHT
    out_shape = [jax.ShapeDtypeStruct(part.shape, jnp.float32)]
    if second:
        copies, spots = chunks
        out_shape.append(jax.ShapeDtypeStruct((copies, spots, bands, planes * rows // spots, columns), jnp.float32))
    halo = pltpu.VMEM((bands, reach, rows, columns), jnp.float32)

    def body(*refs):
        outer_kernel(second, *refs)

    return pl.pallas_call(
        body,
        in_specs=[hbm] * 3,
        out_specs=[hbm] * len(out_shape),
        out_shape=out_shape,
        scratch_shapes=[pltpu.VMEM(part.shape, jnp.float32), halo, halo, pltpu.SemaphoreType.DMA((6 * bands,))],
        compiler_params=pltpu.CompilerParams(vmem_limit_bytes=vmem_bytes),
        cost_estimate=pl.CostEstimate(flops=weight * part.size, bytes_accessed=16 * part.size, transcendentals=0),
        name="outer",
    )(part, lo, hi)


def prepare_kernel(index_ref, panels_ref, sent_ref, low_ref, high_ref, held, sems):
    count, bands, planes, rows, columns = held.shape
    spots, _, height, _ = sent_ref.shape
    arrivals = [pltpu.make_async_copy(panels_ref.at[p], held.at[p], sems.at[p]) for p in range(count)]
    for copy in arrivals:
        copy.start()
    leaving = []

    def leave(source, target):
        copy = pltpu.make_async_copy(source, target, sems.at[count + len(leaving)])
        copy.start()
        leaving.append(copy)

    for p in range(count):
        arrivals[p].wait()
        for b in range(bands):
            leave(held.at[p, b].reshape(spots, height, columns), sent_ref.at[:, p * bands + b])
    block = held.at[index_ref[0]]
    leave(block.at[:, 0:reach], low_ref)
    leave(block.at[:, planes - reach : planes], high_ref)
    for copy in leaving:
        copy.wait()


def prepare(index, panels, spots):
    count, bands, planes, rows, columns = panels.shape
    height = planes * rows // spots
    edge = jax.ShapeDtypeStruct((bands, reach, rows, columns), jnp.float32)
    return pl.pallas_call(
        prepare_kernel,
        in_specs=[pl.BlockSpec(memory_space=pltpu.SMEM), hbm],
        out_specs=[hbm] * 3,
        out_shape=[jax.ShapeDtypeStruct((spots, count * bands, height, columns), jnp.float32), edge, edge],
        scratch_shapes=[pltpu.VMEM(panels.shape, jnp.float32), pltpu.SemaphoreType.DMA((count + count * bands + 2,))],
        compiler_params=pltpu.CompilerParams(vmem_limit_bytes=62 * 1024 * 1024),
        cost_estimate=pl.CostEstimate(flops=0, bytes_accessed=8 * panels.size, transcendentals=0),
        name="prepare",
    )(index, panels)


def settle_kernel(panel_ref, change_ref, out_ref):
    for i in range(change_ref.shape[0]):
        out_ref[:, i] = panel_ref[:, i] - change_ref[i]


def settle(rows, change):
    count, spots = rows.shape[:2]
    step = spots // 2
    mine = pl.BlockSpec((count, step) + rows.shape[2:], lambda i: (0, i, 0, 0))
    return pl.pallas_call(
        settle_kernel,
        grid=(spots // step,),
        in_specs=[mine, pl.BlockSpec((step, count) + rows.shape[2:], lambda i: (i, 0, 0, 0))],
        out_specs=mine,
        out_shape=jax.ShapeDtypeStruct(rows.shape, jnp.float32),
        compiler_params=pltpu.CompilerParams(vmem_limit_bytes=vmem_bytes),
        cost_estimate=pl.CostEstimate(flops=rows.size, bytes_accessed=12 * rows.size, transcendentals=0),
        name="settle",
    )(rows, change)


def split(value):
    high = value.astype(jnp.bfloat16)
    low = (value - high.astype(jnp.float32)).astype(jnp.bfloat16)
    return high, low


def pair(ref, j):
    rows, segments = ref.shape[:2]
    flat = ref.reshape(rows * segments, ref.shape[2])
    first = flat[pl.ds(j, rows, segments), :]
    other = flat[pl.ds(j + segments // 2, rows, segments), :]
    return jnp.concatenate([first, other], axis=1)


def gram_kernel(panel_ref, block_ref, out_ref, total_ref):
    rows, segments = panel_ref.shape[:2]
    bands = block_ref.shape[0]
    contract = (((1,), (1,)), ((), ()))

    def one(j, total):
        panel_high, panel_low = split(pair(panel_ref, j))
        block_high, block_low = split(pair(block_ref, j))
        both = jnp.concatenate([panel_high, panel_low], axis=0)
        wide = lax.dot_general(both, block_high, contract, preferred_element_type=jnp.float32)
        narrow = lax.dot_general(panel_high, block_low, contract, preferred_element_type=jnp.float32)
        return total + (wide[:rows] + (wide[rows:] + narrow))

    @pl.when(pl.program_id(0) == 0)
    def clear():
        total_ref[...] = jnp.zeros_like(total_ref)

    total = lax.fori_loop(0, segments // 2, one, total_ref[...], unroll=8)
    total_ref[...] = total

    @pl.when(pl.program_id(0) == pl.num_programs(0) - 1)
    def store():
        out_ref[...] = jnp.concatenate([total[: rows // 2], total[rows // 2 :]], axis=1)


def gram(panel_rows, block_rows):
    rows, segments, lanes = panel_rows.shape
    bands = block_rows.shape[0]
    steps = 4

    def part(count):
        return pl.BlockSpec((count, segments // steps, lanes), lambda i: (0, i, 0))

    return pl.pallas_call(
        gram_kernel,
        grid=(steps,),
        in_specs=[part(rows), part(bands)],
        out_specs=pl.BlockSpec((rows // 2, 2 * bands), lambda i: (0, 0)),
        out_shape=jax.ShapeDtypeStruct((rows // 2, 2 * bands), jnp.float32),
        scratch_shapes=[pltpu.VMEM((rows, bands), jnp.float32)],
        compiler_params=pltpu.CompilerParams(vmem_limit_bytes=vmem_bytes),
        cost_estimate=pl.CostEstimate(
            flops=6 * bands * panel_rows.size, bytes_accessed=4 * (panel_rows.size + block_rows.size), transcendentals=0
        ),
        name="gram",
    )(panel_rows, block_rows)


def project_kernel(scale, sums_ref, block_ref, out_ref):
    rows, segments, lanes = out_ref.shape
    bands = block_ref.shape[0]
    total = sums_ref[0]
    for i in range(1, sums_ref.shape[0]):
        total = total + sums_ref[i]
    total = total * scale
    corr_high, corr_low = split(jnp.concatenate([total[:, :bands], total[:, bands:]], axis=0))
    left = jnp.concatenate([corr_high, corr_high, corr_low], axis=1)
    flat_out = out_ref.reshape(rows * segments, lanes)
    half = segments // 2

    def one(j, carry):
        high, low = split(pair(block_ref, j))
        product = jnp.dot(left, jnp.concatenate([high, low, high], axis=0), preferred_element_type=jnp.float32)
        flat_out[pl.ds(j, rows, segments), :] = product[:, :lanes]
        flat_out[pl.ds(j + half, rows, segments), :] = product[:, lanes:]
        return carry

    lax.fori_loop(0, half, one, 0, unroll=16)


def project(sums, scale, block_rows):
    rows = 2 * sums.shape[1]
    shape = (rows,) + block_rows.shape[1:]

    def body(*refs):
        project_kernel(scale, *refs)

    return pl.pallas_call(
        body,
        out_shape=jax.ShapeDtypeStruct(shape, jnp.float32),
        compiler_params=pltpu.CompilerParams(vmem_limit_bytes=vmem_bytes),
        cost_estimate=pl.CostEstimate(
            flops=6 * rows * block_rows.size, bytes_accessed=4 * (rows * 8192 + block_rows.size), transcendentals=0
        ),
        name="project",
    )(sums, block_rows)


plane_axes = ("x", "z")


def exchange(low, high):
    up = [(i, (i + 1) % 4) for i in range(4)]
    down = [(j, i) for i, j in up]
    return lax.ppermute(high, ("yh", "c"), up), lax.ppermute(low, ("yh", "c"), down)


def summed(partial, spots):
    parts = [partial]
    for step in range(1, 4):
        parts.append(lax.ppermute(partial, ("yh", "c"), [(i, i ^ step) for i in range(4)]))
    partial = (parts[0] + parts[1]) + (parts[2] + parts[3])
    copies = jnp.broadcast_to(partial[None], (spots,) + partial.shape)
    return lax.all_to_all(copies, plane_axes, 0, 0, tiled=True)


def shards(panels, potential, block_index):
    count, own = panels.shape[:2]
    lanes = panels.shape[-1]
    spots = lax.axis_size(plane_axes)
    cell_count = lax.axis_size("yh") * lax.axis_size("c") * potential.size

    planes = panels.shape[2]
    rows = panels.reshape(count * own, spots, -1, lanes)
    sent, low, high = prepare(block_index, panels, spots)
    before, after = exchange(low, high)
    panel_rows = lax.all_to_all(sent, plane_axes, 0, 0, tiled=True)
    panel_rows = panel_rows.reshape((-1,) + sent.shape[2:])

    (first,) = outer(inner(block_index, panels, potential), before, after)
    before, after = exchange(first[:, :reach], first[:, planes - reach :])
    part = inner(block_index, panels, potential, first)
    filtered, chunks = outer(part, before, after, (lax.axis_size("yl"), spots))
    chunks, panel_rows = lax.optimization_barrier((chunks, panel_rows))
    chunks = chunks.reshape((-1,) + chunks.shape[2:])
    block_rows = lax.all_to_all(
        chunks, ("yl",) + plane_axes, 0, 0, tiled=True
    )
    block_rows = block_rows.reshape((-1,) + chunks.shape[2:])

    sums = summed(gram(panel_rows, block_rows), spots)
    change = project(sums, 1.0 / cell_count, block_rows)
    home = lax.all_to_all(change.reshape(sent.shape), plane_axes, 0, 0, tiled=True)
    updated = settle(rows, home).reshape(panels.shape)
    return filtered, updated


def solution(mesh):
    fine = Mesh(mesh.devices.reshape(4, 4, 2, 2, 2), ("z", "x", "yl", "yh", "c"))
    band, space = ("z", "x", "yl"), ("yh", "c")
    return jax.shard_map(
        shards,
        mesh=fine,
        in_specs=(P(None, band, space, None, None), P(space, None, None), P()),
        out_specs=(P(band, space, None, None), P(None, band, space, None, None)),
        check_vma=False,
    )
```

```python
import jax
import jax.numpy as jnp
from jax import lax
from jax.experimental import pallas as pl
from jax.experimental.pallas import tpu as pltpu
from jax.sharding import Mesh, PartitionSpec as P

stencil_weights = (
    -5369.0 / 1800.0,
    12.0 / 7.0,
    -15.0 / 56.0,
    10.0 / 189.0,
    -1.0 / 112.0,
    2.0 / 1925.0,
    -1.0 / 16632.0,
)
reach = 6
kinetic_factor = -0.5 / 0.25
centre_value = 32.25
half_width = 10.75
vmem_bytes = 16 * 1024 * 1024


def inner_kernel(second, index_ref, panels_ref, pot_ref, *rest):
    if second:
        mid_ref, out_ref, held, held_pot, result_ref, before_ref, sems = rest
    else:
        out_ref, held, held_pot, result_ref, sems = rest
    bands, planes, rows, columns = held.shape
    block_ref = panels_ref.at[index_ref[0]]
    moves = [(pot_ref, held_pot)]
    for b in range(bands):
        moves.append(((mid_ref if second else block_ref).at[b], held.at[b]))
        if second:
            moves.append((block_ref.at[b], before_ref.at[b]))
    copies = [pltpu.make_async_copy(*move, sems.at[i]) for i, move in enumerate(moves)]
    for copy in copies:
        copy.start()
    copies[0].wait()
    scale = (2.0 if second else 1.0) / half_width
    leaving = []
    each = 2 if second else 1
    for b in range(bands):
        for copy in copies[1 + each * b : 1 + each * (b + 1)]:
            copy.wait()
        for z in range(planes):
            centre = held[b, z]
            laplace = 3.0 * stencil_weights[0] * centre
            for k in range(1, reach + 1):
                total = pltpu.roll(centre, k, 0) + pltpu.roll(centre, rows - k, 0)
                total = total + (pltpu.roll(centre, k, 1) + pltpu.roll(centre, columns - k, 1))
                if z + k < planes:
                    total = total + held[b, z + k]
                if z - k >= 0:
                    total = total + held[b, z - k]
                laplace = laplace + stencil_weights[k] * total
            applied = kinetic_factor * laplace + held_pot[z] * centre
            term = (applied - centre_value * centre) * scale
            if second:
                term = term - before_ref[b, z]
            result_ref[b, z] = term
        leaving.append(pltpu.make_async_copy(result_ref.at[b], out_ref.at[b], sems.at[5 + b]))
        leaving[b].start()
    for copy in leaving:
        copy.wait()


def outer_kernel(second, part_ref, lo_ref, hi_ref, out_ref, *rest):
    if second:
        chunk_ref, held, held_lo, held_hi, sems = rest
    else:
        held, held_lo, held_hi, sems = rest
    bands, planes, rows, columns = held.shape
    arrivals = []
    for b in range(bands):
        moves = [(part_ref.at[b], held.at[b]), (lo_ref.at[b], held_lo.at[b]), (hi_ref.at[b], held_hi.at[b])]
        copies = [pltpu.make_async_copy(*move, sems.at[3 * b + i]) for i, move in enumerate(moves)]
        for copy in copies:
            copy.start()
        arrivals.append(copies)
    scale = kinetic_factor * (2.0 if second else 1.0) / half_width
    strip = 16
    leaving = []
    for b in range(bands):
        for copy in arrivals[b]:
            copy.wait()

        def one(i, carry, b=b):
            place = pl.ds(pl.multiple_of(i * strip, strip), strip)
            low = [held_lo[b, j, place] for j in range(reach)]
            high = [held_hi[b, j, place] for j in range(reach)]
            for z in range(planes):
                total = held[b, z, place]
                for k in range(1, reach + 1):
                    if z + k >= planes:
                        total = total + (scale * stencil_weights[k]) * high[z + k - planes]
                    if z - k < 0:
                        total = total + (scale * stencil_weights[k]) * low[reach + z - k]
                held[b, z, place] = total
            return carry

        lax.fori_loop(0, rows // strip, one, 0)
        moves = [(held.at[b], out_ref.at[b])]
        if second:
            copies, depth, width, _, height, _ = chunk_ref.shape
            source = held.at[b].reshape(width, depth, height, columns)
            moves += [(source.at[x], chunk_ref.at[j, :, x, b]) for j in range(copies) for x in range(width)]
        for i, move in enumerate(moves):
            copy = pltpu.make_async_copy(*move, sems.at[3 * bands + len(moves) * b + i])
            copy.start()
            leaving.append(copy)
    for copy in leaving:
        copy.wait()


hbm = pl.BlockSpec(memory_space=pltpu.HBM)
INNER_WEIGHT = 50
OUTER_WEIGHT = 100000


def inner(index, panels, potential, mid=None):
    shape = panels.shape[1:]
    second = mid is not None
    operands = [panels, potential] + ([mid] if second else [])
    held = pltpu.VMEM(shape, jnp.float32)
    scratch = [held, pltpu.VMEM(shape[1:], jnp.float32), held] + ([held] if second else [])

    def body(*refs):
        inner_kernel(second, *refs)

    size = potential.size * shape[0]
    return pl.pallas_call(
        body,
        in_specs=[pl.BlockSpec(memory_space=pltpu.SMEM)] + [hbm] * len(operands),
        out_specs=hbm,
        out_shape=jax.ShapeDtypeStruct(shape, jnp.float32),
        scratch_shapes=scratch + [pltpu.SemaphoreType.DMA((5 + shape[0],))],
        compiler_params=pltpu.CompilerParams(vmem_limit_bytes=vmem_bytes),
        cost_estimate=pl.CostEstimate(
            flops=(50 if second else INNER_WEIGHT) * size, bytes_accessed=12 * size, transcendentals=0
        ),
        name="inner",
    )(index, *operands)


def outer(part, lo, hi, chunks=None):
    bands, planes, rows, columns = part.shape
    second = chunks is not None
    weight = 10 if second else OUTER_WEIGHT
    out_shape = [jax.ShapeDtypeStruct(part.shape, jnp.float32)]
    if second:
        height = planes * rows // (chunks[1] * chunks[2])
        out_shape.append(jax.ShapeDtypeStruct(chunks + (bands, height, columns), jnp.float32))
    halo = pltpu.VMEM((bands, reach, rows, columns), jnp.float32)

    def body(*refs):
        outer_kernel(second, *refs)

    return pl.pallas_call(
        body,
        in_specs=[hbm] * 3,
        out_specs=[hbm] * len(out_shape),
        out_shape=out_shape,
        scratch_shapes=[pltpu.VMEM(part.shape, jnp.float32), halo, halo, pltpu.SemaphoreType.DMA((12 * bands,))],
        compiler_params=pltpu.CompilerParams(vmem_limit_bytes=vmem_bytes),
        cost_estimate=pl.CostEstimate(flops=weight * part.size, bytes_accessed=16 * part.size, transcendentals=0),
        name="outer",
    )(part, lo, hi)


def prepare_kernel(index_ref, panels_ref, sent_ref, low_ref, high_ref, held, sems):
    count, bands, planes, rows, columns = held.shape
    spots, _, height, _ = sent_ref.shape
    arrivals = [pltpu.make_async_copy(panels_ref.at[p], held.at[p], sems.at[p]) for p in range(count)]
    for copy in arrivals:
        copy.start()
    leaving = []

    def leave(source, target):
        copy = pltpu.make_async_copy(source, target, sems.at[count + len(leaving)])
        copy.start()
        leaving.append(copy)

    for p in range(count):
        arrivals[p].wait()
        for b in range(bands):
            leave(held.at[p, b].reshape(spots, height, columns), sent_ref.at[:, p * bands + b])
    block = held.at[index_ref[0]]
    leave(block.at[:, 0:reach], low_ref)
    leave(block.at[:, planes - reach : planes], high_ref)
    for copy in leaving:
        copy.wait()


def prepare(index, panels, spots):
    count, bands, planes, rows, columns = panels.shape
    height = planes * rows // spots
    edge = jax.ShapeDtypeStruct((bands, reach, rows, columns), jnp.float32)
    return pl.pallas_call(
        prepare_kernel,
        in_specs=[pl.BlockSpec(memory_space=pltpu.SMEM), hbm],
        out_specs=[hbm] * 3,
        out_shape=[jax.ShapeDtypeStruct((spots, count * bands, height, columns), jnp.float32), edge, edge],
        scratch_shapes=[pltpu.VMEM(panels.shape, jnp.float32), pltpu.SemaphoreType.DMA((count + count * bands + 2,))],
        compiler_params=pltpu.CompilerParams(vmem_limit_bytes=62 * 1024 * 1024),
        cost_estimate=pl.CostEstimate(flops=0, bytes_accessed=8 * panels.size, transcendentals=0),
        name="prepare",
    )(index, panels)


def settle_kernel(panel_ref, change_ref, out_ref):
    for i in range(change_ref.shape[0]):
        out_ref[:, i] = panel_ref[:, i] - change_ref[i]


def settle(rows, change):
    count, spots = rows.shape[:2]
    step = spots // 2
    mine = pl.BlockSpec((count, step) + rows.shape[2:], lambda i: (0, i, 0, 0))
    return pl.pallas_call(
        settle_kernel,
        grid=(spots // step,),
        in_specs=[mine, pl.BlockSpec((step, count) + rows.shape[2:], lambda i: (i, 0, 0, 0))],
        out_specs=mine,
        out_shape=jax.ShapeDtypeStruct(rows.shape, jnp.float32),
        compiler_params=pltpu.CompilerParams(vmem_limit_bytes=vmem_bytes),
        cost_estimate=pl.CostEstimate(flops=rows.size, bytes_accessed=12 * rows.size, transcendentals=0),
        name="settle",
    )(rows, change)


def split(value):
    high = value.astype(jnp.bfloat16)
    low = (value - high.astype(jnp.float32)).astype(jnp.bfloat16)
    return high, low


def pair(ref, j):
    rows, segments = ref.shape[:2]
    flat = ref.reshape(rows * segments, ref.shape[2])
    first = flat[pl.ds(j, rows, segments), :]
    other = flat[pl.ds(j + segments // 2, rows, segments), :]
    return jnp.concatenate([first, other], axis=1)


def gram_kernel(panel_ref, block_ref, out_ref, total_ref):
    rows, segments = panel_ref.shape[:2]
    bands = block_ref.shape[0]
    contract = (((1,), (1,)), ((), ()))

    def one(j, total):
        panel_high, panel_low = split(pair(panel_ref, j))
        block_high, block_low = split(pair(block_ref, j))
        both = jnp.concatenate([panel_high, panel_low], axis=0)
        wide = lax.dot_general(both, block_high, contract, preferred_element_type=jnp.float32)
        narrow = lax.dot_general(panel_high, block_low, contract, preferred_element_type=jnp.float32)
        return total + (wide[:rows] + (wide[rows:] + narrow))

    @pl.when(pl.program_id(0) == 0)
    def clear():
        total_ref[...] = jnp.zeros_like(total_ref)

    total = lax.fori_loop(0, segments // 2, one, total_ref[...], unroll=8)
    total_ref[...] = total

    @pl.when(pl.program_id(0) == pl.num_programs(0) - 1)
    def store():
        out_ref[...] = jnp.concatenate([total[: rows // 2], total[rows // 2 :]], axis=1)


def gram(panel_rows, block_rows):
    rows, segments, lanes = panel_rows.shape
    bands = block_rows.shape[0]
    steps = 4

    def part(count):
        return pl.BlockSpec((count, segments // steps, lanes), lambda i: (0, i, 0))

    return pl.pallas_call(
        gram_kernel,
        grid=(steps,),
        in_specs=[part(rows), part(bands)],
        out_specs=pl.BlockSpec((rows // 2, 2 * bands), lambda i: (0, 0)),
        out_shape=jax.ShapeDtypeStruct((rows // 2, 2 * bands), jnp.float32),
        scratch_shapes=[pltpu.VMEM((rows, bands), jnp.float32)],
        compiler_params=pltpu.CompilerParams(vmem_limit_bytes=vmem_bytes),
        cost_estimate=pl.CostEstimate(
            flops=6 * bands * panel_rows.size, bytes_accessed=4 * (panel_rows.size + block_rows.size), transcendentals=0
        ),
        name="gram",
    )(panel_rows, block_rows)


def project_kernel(scale, sums_ref, block_ref, out_ref):
    rows, segments, lanes = out_ref.shape
    bands = block_ref.shape[0]
    total = sums_ref[0]
    for i in range(1, sums_ref.shape[0]):
        total = total + sums_ref[i]
    total = total * scale
    corr_high, corr_low = split(jnp.concatenate([total[:, :bands], total[:, bands:]], axis=0))
    left = jnp.concatenate([corr_high, corr_high, corr_low], axis=1)
    flat_out = out_ref.reshape(rows * segments, lanes)
    half = segments // 2

    def one(j, carry):
        high, low = split(pair(block_ref, j))
        product = jnp.dot(left, jnp.concatenate([high, low, high], axis=0), preferred_element_type=jnp.float32)
        flat_out[pl.ds(j, rows, segments), :] = product[:, :lanes]
        flat_out[pl.ds(j + half, rows, segments), :] = product[:, lanes:]
        return carry

    lax.fori_loop(0, half, one, 0, unroll=16)


def project(sums, scale, block_rows):
    rows = 2 * sums.shape[1]
    shape = (rows,) + block_rows.shape[1:]

    def body(*refs):
        project_kernel(scale, *refs)

    return pl.pallas_call(
        body,
        out_shape=jax.ShapeDtypeStruct(shape, jnp.float32),
        compiler_params=pltpu.CompilerParams(vmem_limit_bytes=vmem_bytes),
        cost_estimate=pl.CostEstimate(
            flops=6 * rows * block_rows.size, bytes_accessed=4 * (rows * 8192 + block_rows.size), transcendentals=0
        ),
        name="project",
    )(sums, block_rows)


plane_axes = ("x", "z")


def exchange(low, high):
    up = [(i, (i + 1) % 4) for i in range(4)]
    down = [(j, i) for i, j in up]
    return lax.ppermute(high, ("yh", "c"), up), lax.ppermute(low, ("yh", "c"), down)


def summed(partial, spots):
    parts = [partial]
    for step in range(1, 4):
        parts.append(lax.ppermute(partial, ("yh", "c"), [(i, i ^ step) for i in range(4)]))
    partial = (parts[0] + parts[1]) + (parts[2] + parts[3])
    copies = jnp.broadcast_to(partial[None], (spots,) + partial.shape)
    return lax.all_to_all(copies, plane_axes, 0, 0, tiled=True)


def shards(panels, potential, block_index):
    count, own = panels.shape[:2]
    lanes = panels.shape[-1]
    spots = lax.axis_size(plane_axes)
    cell_count = lax.axis_size("yh") * lax.axis_size("c") * potential.size

    planes = panels.shape[2]
    rows = panels.reshape(count * own, spots, -1, lanes)
    sent, low, high = prepare(block_index, panels, spots)
    before, after = exchange(low, high)
    panel_rows = lax.all_to_all(sent, plane_axes, 0, 0, tiled=True)
    panel_rows = panel_rows.reshape((-1,) + sent.shape[2:])

    (first,) = outer(inner(block_index, panels, potential), before, after)
    before, after = exchange(first[:, :reach], first[:, planes - reach :])
    part = inner(block_index, panels, potential, first)
    filtered, chunks = outer(part, before, after, tuple(lax.axis_size(axis) for axis in ("yl", "z", "x")))
    chunks, panel_rows = lax.optimization_barrier((chunks, panel_rows))
    chunks = chunks.reshape((-1,) + chunks.shape[3:])
    block_rows = lax.all_to_all(
        chunks, ("yl", "z", "x"), 0, 0, tiled=True
    )
    block_rows = block_rows.reshape((-1,) + chunks.shape[2:])

    sums = summed(gram(panel_rows, block_rows), spots)
    change = project(sums, 1.0 / cell_count, block_rows)
    home = lax.all_to_all(change.reshape(sent.shape), plane_axes, 0, 0, tiled=True)
    updated = settle(rows, home).reshape(panels.shape)
    return filtered, updated


def solution(mesh):
    fine = Mesh(mesh.devices.reshape(4, 4, 2, 2, 2), ("z", "x", "yl", "yh", "c"))
    band, space = ("z", "x", "yl"), ("yh", "c")
    return jax.shard_map(
        shards,
        mesh=fine,
        in_specs=(P(None, band, space, None, None), P(space, None, None), P()),
        out_specs=(P(band, space, None, None), P(None, band, space, None, None)),
        check_vma=False,
    )
```

```python
import jax
import jax.numpy as jnp
from jax import lax
from jax.experimental import pallas as pl
from jax.experimental.pallas import tpu as pltpu
from jax.sharding import Mesh, PartitionSpec as P

stencil_weights = (
    -5369.0 / 1800.0,
    12.0 / 7.0,
    -15.0 / 56.0,
    10.0 / 189.0,
    -1.0 / 112.0,
    2.0 / 1925.0,
    -1.0 / 16632.0,
)
reach = 6
kinetic_factor = -0.5 / 0.25
centre_value = 32.25
half_width = 10.75
vmem_bytes = 16 * 1024 * 1024


def inner_kernel(second, index_ref, panels_ref, pot_ref, *rest):
    if second:
        mid_ref, out_ref, held, held_pot, result_ref, before_ref, sems = rest
    else:
        out_ref, held, held_pot, result_ref, sems = rest
    bands, planes, rows, columns = held.shape
    block_ref = panels_ref.at[index_ref[0]]
    moves = [(pot_ref, held_pot)]
    for b in range(bands):
        moves.append(((mid_ref if second else block_ref).at[b], held.at[b]))
        if second:
            moves.append((block_ref.at[b], before_ref.at[b]))
    copies = [pltpu.make_async_copy(*move, sems.at[i]) for i, move in enumerate(moves)]
    for copy in copies:
        copy.start()
    copies[0].wait()
    scale = (2.0 if second else 1.0) / half_width
    leaving = []
    each = 2 if second else 1
    for b in range(bands):
        for copy in copies[1 + each * b : 1 + each * (b + 1)]:
            copy.wait()
        for z in range(planes):
            centre = held[b, z]
            laplace = 3.0 * stencil_weights[0] * centre
            for k in range(1, reach + 1):
                total = pltpu.roll(centre, k, 0) + pltpu.roll(centre, rows - k, 0)
                total = total + (pltpu.roll(centre, k, 1) + pltpu.roll(centre, columns - k, 1))
                if z + k < planes:
                    total = total + held[b, z + k]
                if z - k >= 0:
                    total = total + held[b, z - k]
                laplace = laplace + stencil_weights[k] * total
            applied = kinetic_factor * laplace + held_pot[z] * centre
            term = (applied - centre_value * centre) * scale
            if second:
                term = term - before_ref[b, z]
            result_ref[b, z] = term
        leaving.append(pltpu.make_async_copy(result_ref.at[b], out_ref.at[b], sems.at[5 + b]))
        leaving[b].start()
    for copy in leaving:
        copy.wait()


def outer_kernel(second, part_ref, lo_ref, hi_ref, out_ref, *rest):
    if second:
        chunk_ref, held, held_lo, held_hi, sems = rest
    else:
        held, held_lo, held_hi, sems = rest
    bands, planes, rows, columns = held.shape
    arrivals = []
    for b in range(bands):
        moves = [(part_ref.at[b], held.at[b]), (lo_ref.at[b], held_lo.at[b]), (hi_ref.at[b], held_hi.at[b])]
        copies = [pltpu.make_async_copy(*move, sems.at[3 * b + i]) for i, move in enumerate(moves)]
        for copy in copies:
            copy.start()
        arrivals.append(copies)
    scale = kinetic_factor * (2.0 if second else 1.0) / half_width
    strip = 16
    leaving = []
    for b in range(bands):
        for copy in arrivals[b]:
            copy.wait()

        def one(i, carry, b=b):
            place = pl.ds(pl.multiple_of(i * strip, strip), strip)
            low = [held_lo[b, j, place] for j in range(reach)]
            high = [held_hi[b, j, place] for j in range(reach)]
            for z in range(planes):
                total = held[b, z, place]
                for k in range(1, reach + 1):
                    if z + k >= planes:
                        total = total + (scale * stencil_weights[k]) * high[z + k - planes]
                    if z - k < 0:
                        total = total + (scale * stencil_weights[k]) * low[reach + z - k]
                held[b, z, place] = total
            return carry

        lax.fori_loop(0, rows // strip, one, 0)
        moves = [(held.at[b], out_ref.at[b])]
        if second:
            copies, depth, width, _, height, _ = chunk_ref.shape
            source = held.at[b].reshape(width, depth, height, columns)
            moves += [(source.at[x], chunk_ref.at[j, :, x, b]) for j in range(copies) for x in range(width)]
        for i, move in enumerate(moves):
            copy = pltpu.make_async_copy(*move, sems.at[3 * bands + len(moves) * b + i])
            copy.start()
            leaving.append(copy)
    for copy in leaving:
        copy.wait()


hbm = pl.BlockSpec(memory_space=pltpu.HBM)
INNER_WEIGHT = 50
OUTER_WEIGHT = 100000


def inner(index, panels, potential, mid=None):
    shape = panels.shape[1:]
    second = mid is not None
    operands = [panels, potential] + ([mid] if second else [])
    held = pltpu.VMEM(shape, jnp.float32)
    scratch = [held, pltpu.VMEM(shape[1:], jnp.float32), held] + ([held] if second else [])

    def body(*refs):
        inner_kernel(second, *refs)

    size = potential.size * shape[0]
    return pl.pallas_call(
        body,
        in_specs=[pl.BlockSpec(memory_space=pltpu.SMEM)] + [hbm] * len(operands),
        out_specs=hbm,
        out_shape=jax.ShapeDtypeStruct(shape, jnp.float32),
        scratch_shapes=scratch + [pltpu.SemaphoreType.DMA((5 + shape[0],))],
        compiler_params=pltpu.CompilerParams(vmem_limit_bytes=vmem_bytes),
        cost_estimate=pl.CostEstimate(
            flops=(50 if second else INNER_WEIGHT) * size, bytes_accessed=12 * size, transcendentals=0
        ),
        name="inner",
    )(index, *operands)


def outer(part, lo, hi, chunks=None):
    bands, planes, rows, columns = part.shape
    second = chunks is not None
    weight = 10 if second else OUTER_WEIGHT
    out_shape = [jax.ShapeDtypeStruct(part.shape, jnp.float32)]
    if second:
        height = planes * rows // (chunks[1] * chunks[2])
        out_shape.append(jax.ShapeDtypeStruct(chunks + (bands, height, columns), jnp.float32))
    halo = pltpu.VMEM((bands, reach, rows, columns), jnp.float32)

    def body(*refs):
        outer_kernel(second, *refs)

    return pl.pallas_call(
        body,
        in_specs=[hbm] * 3,
        out_specs=[hbm] * len(out_shape),
        out_shape=out_shape,
        scratch_shapes=[pltpu.VMEM(part.shape, jnp.float32), halo, halo, pltpu.SemaphoreType.DMA((12 * bands,))],
        compiler_params=pltpu.CompilerParams(vmem_limit_bytes=vmem_bytes),
        cost_estimate=pl.CostEstimate(flops=weight * part.size, bytes_accessed=16 * part.size, transcendentals=0),
        name="outer",
    )(part, lo, hi)


def prepare_kernel(index_ref, panels_ref, sent_ref, low_ref, high_ref, held, sems):
    count, bands, planes, rows, columns = held.shape
    spots, _, height, _ = sent_ref.shape
    arrivals = [pltpu.make_async_copy(panels_ref.at[p], held.at[p], sems.at[p]) for p in range(count)]
    for copy in arrivals:
        copy.start()
    leaving = []

    def leave(source, target):
        copy = pltpu.make_async_copy(source, target, sems.at[count + len(leaving)])
        copy.start()
        leaving.append(copy)

    for p in range(count):
        arrivals[p].wait()
        for b in range(bands):
            leave(held.at[p, b].reshape(spots, height, columns), sent_ref.at[:, p * bands + b])
    block = held.at[index_ref[0]]
    leave(block.at[:, 0:reach], low_ref)
    leave(block.at[:, planes - reach : planes], high_ref)
    for copy in leaving:
        copy.wait()


def prepare(index, panels, spots):
    count, bands, planes, rows, columns = panels.shape
    height = planes * rows // spots
    edge = jax.ShapeDtypeStruct((bands, reach, rows, columns), jnp.float32)
    return pl.pallas_call(
        prepare_kernel,
        in_specs=[pl.BlockSpec(memory_space=pltpu.SMEM), hbm],
        out_specs=[hbm] * 3,
        out_shape=[jax.ShapeDtypeStruct((spots, count * bands, height, columns), jnp.float32), edge, edge],
        scratch_shapes=[pltpu.VMEM(panels.shape, jnp.float32), pltpu.SemaphoreType.DMA((count + count * bands + 2,))],
        compiler_params=pltpu.CompilerParams(vmem_limit_bytes=62 * 1024 * 1024),
        cost_estimate=pl.CostEstimate(flops=0, bytes_accessed=8 * panels.size, transcendentals=0),
        name="prepare",
    )(index, panels)


def settle_kernel(panel_ref, change_ref, out_ref, held, sems):
    spots = change_ref.shape[0]
    step = spots // 4
    leaving = []
    for part in range(4):
        for i in range(part * step, (part + 1) * step):
            held[:, i] = panel_ref[:, i] - change_ref[i]
        place = pl.ds(part * step, step)
        leaving.append(pltpu.make_async_copy(held.at[:, place], out_ref.at[:, place], sems.at[part]))
        leaving[part].start()
    for copy in leaving:
        copy.wait()


def settle(rows, change):
    whole = pl.BlockSpec(memory_space=pltpu.VMEM)
    return pl.pallas_call(
        settle_kernel,
        in_specs=[whole, whole],
        out_specs=hbm,
        out_shape=jax.ShapeDtypeStruct(rows.shape, jnp.float32),
        scratch_shapes=[pltpu.VMEM(rows.shape, jnp.float32), pltpu.SemaphoreType.DMA((4,))],
        compiler_params=pltpu.CompilerParams(vmem_limit_bytes=vmem_bytes),
        cost_estimate=pl.CostEstimate(flops=rows.size, bytes_accessed=12 * rows.size, transcendentals=0),
        name="settle",
    )(rows, change)


def split(value):
    high = value.astype(jnp.bfloat16)
    low = (value - high.astype(jnp.float32)).astype(jnp.bfloat16)
    return high, low


def pair(ref, j):
    rows, segments = ref.shape[:2]
    flat = ref.reshape(rows * segments, ref.shape[2])
    first = flat[pl.ds(j, rows, segments), :]
    other = flat[pl.ds(j + segments // 2, rows, segments), :]
    return jnp.concatenate([first, other], axis=1)


def gram_kernel(panel_ref, block_ref, out_ref, total_ref):
    rows, segments = panel_ref.shape[:2]
    bands = block_ref.shape[0]
    contract = (((1,), (1,)), ((), ()))

    def one(j, total):
        panel_high, panel_low = split(pair(panel_ref, j))
        block_high, block_low = split(pair(block_ref, j))
        both = jnp.concatenate([panel_high, panel_low], axis=0)
        wide = lax.dot_general(both, block_high, contract, preferred_element_type=jnp.float32)
        narrow = lax.dot_general(panel_high, block_low, contract, preferred_element_type=jnp.float32)
        return total + (wide[:rows] + (wide[rows:] + narrow))

    @pl.when(pl.program_id(0) == 0)
    def clear():
        total_ref[...] = jnp.zeros_like(total_ref)

    total = lax.fori_loop(0, segments // 2, one, total_ref[...], unroll=8)
    total_ref[...] = total

    @pl.when(pl.program_id(0) == pl.num_programs(0) - 1)
    def store():
        out_ref[...] = jnp.concatenate([total[: rows // 2], total[rows // 2 :]], axis=1)


def gram(panel_rows, block_rows):
    rows, segments, lanes = panel_rows.shape
    bands = block_rows.shape[0]
    steps = 4

    def part(count):
        return pl.BlockSpec((count, segments // steps, lanes), lambda i: (0, i, 0))

    return pl.pallas_call(
        gram_kernel,
        grid=(steps,),
        in_specs=[part(rows), part(bands)],
        out_specs=pl.BlockSpec((rows // 2, 2 * bands), lambda i: (0, 0)),
        out_shape=jax.ShapeDtypeStruct((rows // 2, 2 * bands), jnp.float32),
        scratch_shapes=[pltpu.VMEM((rows, bands), jnp.float32)],
        compiler_params=pltpu.CompilerParams(vmem_limit_bytes=vmem_bytes),
        cost_estimate=pl.CostEstimate(
            flops=6 * bands * panel_rows.size, bytes_accessed=4 * (panel_rows.size + block_rows.size), transcendentals=0
        ),
        name="gram",
    )(panel_rows, block_rows)


def project_kernel(scale, sums_ref, block_ref, out_ref):
    rows, segments, lanes = out_ref.shape
    bands = block_ref.shape[0]
    total = sums_ref[0]
    for i in range(1, sums_ref.shape[0]):
        total = total + sums_ref[i]
    total = total * scale
    corr_high, corr_low = split(jnp.concatenate([total[:, :bands], total[:, bands:]], axis=0))
    left = jnp.concatenate([corr_high, corr_high, corr_low], axis=1)
    flat_out = out_ref.reshape(rows * segments, lanes)
    half = segments // 2

    def one(j, carry):
        high, low = split(pair(block_ref, j))
        product = jnp.dot(left, jnp.concatenate([high, low, high], axis=0), preferred_element_type=jnp.float32)
        flat_out[pl.ds(j, rows, segments), :] = product[:, :lanes]
        flat_out[pl.ds(j + half, rows, segments), :] = product[:, lanes:]
        return carry

    lax.fori_loop(0, half, one, 0, unroll=16)


def project(sums, scale, block_rows):
    rows = 2 * sums.shape[1]
    shape = (rows,) + block_rows.shape[1:]

    def body(*refs):
        project_kernel(scale, *refs)

    return pl.pallas_call(
        body,
        out_shape=jax.ShapeDtypeStruct(shape, jnp.float32),
        compiler_params=pltpu.CompilerParams(vmem_limit_bytes=vmem_bytes),
        cost_estimate=pl.CostEstimate(
            flops=6 * rows * block_rows.size, bytes_accessed=4 * (rows * 8192 + block_rows.size), transcendentals=0
        ),
        name="project",
    )(sums, block_rows)


plane_axes = ("x", "z")


def exchange(low, high):
    up = [(i, (i + 1) % 4) for i in range(4)]
    down = [(j, i) for i, j in up]
    return lax.ppermute(high, ("yh", "c"), up), lax.ppermute(low, ("yh", "c"), down)


def summed(partial, spots):
    parts = [partial]
    for step in range(1, 4):
        parts.append(lax.ppermute(partial, ("yh", "c"), [(i, i ^ step) for i in range(4)]))
    partial = (parts[0] + parts[1]) + (parts[2] + parts[3])
    copies = jnp.broadcast_to(partial[None], (spots,) + partial.shape)
    return lax.all_to_all(copies, plane_axes, 0, 0, tiled=True)


def shards(panels, potential, block_index):
    count, own = panels.shape[:2]
    lanes = panels.shape[-1]
    spots = lax.axis_size(plane_axes)
    cell_count = lax.axis_size("yh") * lax.axis_size("c") * potential.size

    planes = panels.shape[2]
    rows = panels.reshape(count * own, spots, -1, lanes)
    sent, low, high = prepare(block_index, panels, spots)
    before, after = exchange(low, high)
    panel_rows = lax.all_to_all(sent, plane_axes, 0, 0, tiled=True)
    panel_rows = panel_rows.reshape((-1,) + sent.shape[2:])

    (first,) = outer(inner(block_index, panels, potential), before, after)
    before, after = exchange(first[:, :reach], first[:, planes - reach :])
    part = inner(block_index, panels, potential, first)
    filtered, chunks = outer(part, before, after, tuple(lax.axis_size(axis) for axis in ("yl", "z", "x")))
    chunks, panel_rows = lax.optimization_barrier((chunks, panel_rows))
    chunks = chunks.reshape((-1,) + chunks.shape[3:])
    block_rows = lax.all_to_all(
        chunks, ("yl", "z", "x"), 0, 0, tiled=True
    )
    block_rows = block_rows.reshape((-1,) + chunks.shape[2:])

    sums = summed(gram(panel_rows, block_rows), spots)
    change = project(sums, 1.0 / cell_count, block_rows)
    home = lax.all_to_all(change.reshape(sent.shape), plane_axes, 0, 0, tiled=True)
    updated = settle(rows, home).reshape(panels.shape)
    return filtered, updated


def solution(mesh):
    fine = Mesh(mesh.devices.reshape(4, 4, 2, 2, 2), ("z", "x", "yl", "yh", "c"))
    band, space = ("z", "x", "yl"), ("yh", "c")
    return jax.shard_map(
        shards,
        mesh=fine,
        in_specs=(P(None, band, space, None, None), P(space, None, None), P()),
        out_specs=(P(band, space, None, None), P(None, band, space, None, None)),
        check_vma=False,
    )
```
